32 devices in a mesh: dp: 8 (over z, core), tm: 4 (over y, x).
Axes of the slice: x: 2, y: 2, z: 4, core: 2. Of those that a mesh axis runs over, the one named last changes fastest.
Arguments:
- video_tokens: bfloat16 [8, 32, 196, 768], P('dp', 'tm'), may hold values from -6 to 6
- norm_gain: bfloat16 [768], P('dp'), may hold values from 0.25 to 1.75
- norm_bias: bfloat16 [768], P('dp'), may hold values from -3 to 3
- qkv_weight: bfloat16 [768, 1152], P('dp'), may hold values from -16 to 16
- frame_counts: int32 [8], P('dp'), may hold values from 16 to 32, as said below
- clip_starts: int32 [8, 2], P('dp'), may hold values 0 or 1
- frame_kept: int32 [8, 32], P('dp'), may hold values 0 or 1
- attended_grad: bfloat16 [8, 32, 196, 384], P('dp', 'tm'), may hold values from -6 to 6
Outputs:
- attended: bfloat16 [8, 32, 196, 384], P('dp', 'tm')
- tokens_grad: bfloat16 [8, 32, 196, 768], P('dp', 'tm')
- qkv_weight_grad: float32 [768, 1152], P('dp')
- gain_grad: float32 [768], P('dp')
- bias_grad: float32 [768], P('dp')
The draws below stay inside these ranges and needn't reach their ends.
Inputs may be any that keep to these rules, and one draw needn't show every extreme that they name: `frame_counts`: every count is a multiple of 16; some video has 32 frames and some video has 16.
All inputs are finite; a program needn't handle non-finite values. No bound on the sum of `clip_starts` or of `frame_kept` on one device may be relied on, other than what follows from the above.
Results may differ from the reference program's by a relative error of at most 0.02.
Values may be sent and summed in bfloat16 or wider, within the bound.
No kernel may reach another device: no remote copies, remote signals or barrier semaphores. Data moves between devices by JAX's collectives and lax.ppermute only.
A program may use at most 128 MiB of HBM per device.

```python
import jax
import jax.numpy as jnp
from jax import lax

D = 768
HEADS = 6
PATCHES = 196
BLOCK = 16
HD = 384
FRAMES = 32
NB = 2
VIDEOS = 8


def draw_qkv_weight(key, part):
    normal_part = jax.random.normal(jax.random.fold_in(key, 11), (D, 3 * HD), jnp.float32) * D ** (-0.5)
    return jnp.clip(normal_part, -16.0, 16.0).astype(jnp.bfloat16)


def draw_frame_counts(key, part):
    blocks = jax.random.randint(jax.random.fold_in(key, 21), (VIDEOS,), 1, NB + 1)
    order = jax.random.permutation(jax.random.fold_in(key, 22), VIDEOS)
    blocks = blocks.at[order[0]].set(NB)
    blocks = blocks.at[order[1]].set(1)
    return (blocks * BLOCK).astype(jnp.int32)


def place_ends(values, stream_key, least, largest):
    extent = values.shape
    spot = [jax.random.randint(jax.random.fold_in(stream_key, axis), (), 0, extent[axis]) for axis in range(len(extent))]
    values = values.at[tuple(spot)].set(least)
    longest = extent.index(max(extent))
    spot[longest] = (spot[longest] + 1) % extent[longest]
    return values.at[tuple(spot)].set(largest)


def strengthened(array, rng, source, target, blocks, factor):
    owner, partner = [(jnp.arange(array.shape[position]) // (array.shape[position] // blocks)).reshape([-1 if axis == position else 1 for axis in range(array.ndim)]) for position in (source, target)]
    chosen = jax.random.permutation(rng, blocks)[partner]
    strong = (owner == chosen) | (owner == (partner + blocks // 2) % blocks)
    return jnp.where(strong, factor * array, array)


def level_of(key, extent, cuts, low, high):
    loudness = 1.0
    for dim, blocks in cuts:
        heights = jax.random.uniform(jax.random.fold_in(jax.random.fold_in(key, 6), dim), (blocks,), jnp.float32, low / len(cuts), high / len(cuts))
        loudness = loudness * jnp.repeat(jnp.exp(heights), extent[dim] // blocks).reshape((-1,) + (1,) * (len(extent) - 1 - dim))
    return loudness


def gaussian(stream_key, shape, scale, reach, split=(), kind=jnp.bfloat16):
    drawn = jax.random.normal(stream_key, shape, jnp.float32) * scale
    if len(split) > 0:
        drawn = level_of(stream_key, shape, split, -0.22, 0.18) * drawn
    return jnp.clip(drawn, min=-reach, max=reach).astype(kind)


def heavy_noise(stream_key, dims, scale, reach, pieces, heavy, kind=jnp.bfloat16):
    array = scale * jax.random.normal(stream_key, dims, jnp.float32)
    if pieces:
        array = array * level_of(stream_key, dims, pieces, -0.22, 0.18)
    return jnp.clip(strengthened(array, jax.random.fold_in(stream_key, 3), *heavy), -reach, reach).astype(kind)


def setup_inputs(seed: int = 0) -> dict:
    splits = jax.random.split(jax.random.key(seed), 9)
    video_tokens = heavy_noise(splits[0], (VIDEOS, FRAMES, PATCHES, D), 1.0, 6.0, ((0, 8), (1, 4)), (0, 3, 8, 2.0))
    norm_gain = jnp.clip(1.0 + 0.15 * jax.random.normal(splits[1], (D,), jnp.float32), 0.25, 1.75).astype(jnp.bfloat16)
    norm_bias = gaussian(splits[2], (D,), 0.5, 3.0, ((0, 8),))
    qkv_weight = draw_qkv_weight(jax.random.fold_in(splits[8], 71), 0)
    frame_counts = draw_frame_counts(jax.random.fold_in(splits[8], 71), 0)
    clip_starts = place_ends((jax.random.randint(splits[5], (VIDEOS, NB), 0, 3) < 1).astype(jnp.int32), jax.random.fold_in(splits[5], 1), 0, 1)
    frame_kept = place_ends((jax.random.randint(splits[6], (VIDEOS, FRAMES), 0, 8) < 7).astype(jnp.int32), jax.random.fold_in(splits[6], 1), 0, 1)
    attended_grad = gaussian(splits[7], (VIDEOS, FRAMES, PATCHES, HD), 1.0, 6.0, ((0, 8), (1, 4)))
    return dict(video_tokens=video_tokens, norm_gain=norm_gain, norm_bias=norm_bias, qkv_weight=qkv_weight, frame_counts=frame_counts, clip_starts=clip_starts, frame_kept=frame_kept, attended_grad=attended_grad)


masked_value = -1e+30
epsilon = 1e-05

def standardize(rows):
    centred = rows - lax.optimization_barrier(jnp.mean(rows, axis=-1, keepdims=True))
    inverse = lax.rsqrt(lax.optimization_barrier(jnp.mean(centred * centred, axis=-1, keepdims=True)) + epsilon)
    return (centred * inverse, inverse)

def frame_masks(frame_count, starts, kept, frames):
    frame_index = jnp.arange(frames, dtype=jnp.int32)
    block_index = jnp.arange(starts.shape[0], dtype=jnp.int32)
    flags = jnp.where(block_index > 0, starts, 0)
    clip_of_block = jnp.cumsum(flags).astype(jnp.int32)
    clip_number = clip_of_block[(frame_index // BLOCK).astype(jnp.int32)]
    usable = (frame_index < frame_count) & (kept == 1)
    same_clip = clip_number[:, None] == clip_number[None, :]
    allowed = same_clip & (usable[None, :] | (frame_index[:, None] == frame_index[None, :]))
    return (allowed, frame_index < frame_count)

def split_heads(projected, start, joined):
    return projected[:, :, start:start + joined].reshape(projected.shape[0], projected.shape[1], HEADS, joined // HEADS).astype(jnp.float32)

def attend(projected, allowed, valid):
    frames, patch_rows = (projected.shape[0], projected.shape[1])
    joined = projected.shape[2] // 3
    scale = (joined // HEADS) ** (-0.5)
    queries = split_heads(projected, 0, joined)
    key_rows = split_heads(projected, joined, joined)
    values = split_heads(projected, 2 * joined, joined)
    scores = jnp.einsum('fphd,gphd->phfg', queries, key_rows) * scale
    scores = jnp.where(allowed, scores, masked_value)
    shifted = jnp.exp(scores - lax.optimization_barrier(jnp.max(scores, axis=-1, keepdims=True)))
    weights = shifted / lax.optimization_barrier(jnp.sum(shifted, axis=-1, keepdims=True))
    rounded = weights.astype(jnp.bfloat16).astype(jnp.float32)
    mixed = jnp.einsum('phfg,gphd->fphd', rounded, values)
    mixed = jnp.where(valid[:, None, None, None], mixed, 0.0)
    return (mixed.reshape(frames, patch_rows, joined).astype(jnp.bfloat16), weights)

def attend_back(projected, weights, upstream, valid):
    frames, patch_rows = (projected.shape[0], projected.shape[1])
    joined = projected.shape[2] // 3
    head_width = joined // HEADS
    scale = head_width ** (-0.5)
    queries = split_heads(projected, 0, joined)
    key_rows = split_heads(projected, joined, joined)
    values = split_heads(projected, 2 * joined, joined)
    kept_grad = jnp.where(valid[:, None, None], upstream, jnp.zeros_like(upstream))
    kept_grad = kept_grad.reshape(frames, patch_rows, HEADS, head_width).astype(jnp.float32)
    rounded = weights.astype(jnp.bfloat16).astype(jnp.float32)
    weight_grad = jnp.einsum('fphd,gphd->phfg', kept_grad, values)
    value_grad = jnp.einsum('phfg,fphd->gphd', rounded, kept_grad)
    inner = lax.optimization_barrier(jnp.sum(weight_grad * weights, axis=-1, keepdims=True))
    score_grad = (weights * (weight_grad - inner) * scale).astype(jnp.bfloat16).astype(jnp.float32)
    query_grad = jnp.einsum('phfg,gphd->fphd', score_grad, key_rows)
    key_grad = jnp.einsum('phfg,fphd->gphd', score_grad, queries)
    parts = [query_grad, key_grad, value_grad]
    return jnp.concatenate([piece.reshape(frames, patch_rows, joined) for piece in parts], axis=2).astype(jnp.bfloat16)

def reference(video_tokens, norm_gain, norm_bias, qkv_weight, frame_counts, clip_starts, frame_kept, attended_grad):
    gain_wide = norm_gain.astype(jnp.float32)
    bias_wide = norm_bias.astype(jnp.float32)
    columns = qkv_weight.shape[1]

    def one_video(carry, inputs):
        tokens, frame_count, starts, kept, upstream = inputs
        frames, patches, model_width = tokens.shape
        standard, inverse = standardize(tokens.reshape(-1, model_width).astype(jnp.float32))
        normed = (standard * gain_wide + bias_wide).astype(jnp.bfloat16)
        projected = jnp.dot(normed, qkv_weight, preferred_element_type=jnp.float32).astype(jnp.bfloat16)
        projected = projected.reshape(frames, patches, columns)
        allowed, valid = frame_masks(frame_count, starts, kept, frames)
        mixed, weights = attend(projected, allowed, valid)
        projected_grad = attend_back(projected, weights, upstream, valid).reshape(-1, columns)
        weight_grad = lax.dot_general(normed, projected_grad, (((0,), (0,)), ((), ())), preferred_element_type=jnp.float32)
        normed_grad = lax.dot_general(projected_grad, qkv_weight, (((1,), (1,)), ((), ())), preferred_element_type=jnp.float32)
        normed_grad = lax.optimization_barrier(normed_grad.astype(jnp.bfloat16)).astype(jnp.float32)
        gain_part = lax.optimization_barrier(jnp.sum(normed_grad * standard, axis=0))
        bias_part = lax.optimization_barrier(jnp.sum(normed_grad, axis=0))
        scaled = normed_grad * gain_wide
        tokens_grad = inverse * (scaled - lax.optimization_barrier(jnp.mean(scaled, axis=-1, keepdims=True)) - standard * lax.optimization_barrier(jnp.mean(scaled * standard, axis=-1, keepdims=True)))
        tokens_grad = tokens_grad.astype(jnp.bfloat16).reshape(frames, patches, model_width)
        total_w, total_gain, total_bias = carry
        return ((total_w + weight_grad, total_gain + gain_part, total_bias + bias_part), (mixed, tokens_grad))
    start = (jnp.zeros(qkv_weight.shape, jnp.float32), jnp.zeros(norm_gain.shape, jnp.float32), jnp.zeros(norm_bias.shape, jnp.float32))
    sums, stacked = lax.scan(one_video, start, (video_tokens, frame_counts, clip_starts, frame_kept, attended_grad))
    return (stacked[0], stacked[1], sums[0], sums[1], sums[2])
```

```python
import functools

import jax
import jax.numpy as jnp
from jax import lax
from jax.experimental import pallas as pl
from jax.experimental.pallas import tpu as pltpu
from jax.sharding import PartitionSpec as P

HEADS = 6
BLOCK = 16
CORES = 2
EXTRA = 16

masked_value = -1e30
epsilon = 1e-05
vmem_limit = 56 * 1024 * 1024
f32 = jnp.float32
bf16 = jnp.bfloat16


def round_up(value, step):
    return -(-value // step) * step


def chunk_sizes(patches_dev, group, count):
    groups = -(-patches_dev // group)
    count = min(count, groups)
    sizes = []
    left = patches_dev
    for index in range(count - 1):
        taken = (groups // count) * group
        sizes.append((taken, taken))
        left -= taken
    sizes.append((left, round_up(left, 2)))
    return sizes


def pack_kernel(
    tm_count, patches_dev, offset, real, sent, padded, x_ref, grad_ref, *rest
):
    outs, wide = rest[:-1], rest[-1]
    frames, patches, width = x_ref.shape[1:]
    me = lax.axis_index("tm")
    lanes = wide.shape[0]
    for f in range(frames):
        for c in range(lanes):
            at = c * 128
            ref, at = (x_ref, at) if at < width else (grad_ref, at - width)
            wide[c, f * padded : f * padded + patches] = ref[0, f, :, at : at + 128].astype(f32)
            if padded > patches:
                wide[c, f * padded + patches : (f + 1) * padded] = jnp.zeros(
                    (padded - patches, 128), f32
                )
    for r in range(tm_count):
        base = (me ^ r) * patches_dev + offset

        def two(k, base=base, out=outs[r]):
            place = pl.ds(pl.multiple_of(k * 2 * frames, 2 * frames), 2 * frames)
            for c in range(lanes):
                rows = []
                for i in range(2):
                    q = 2 * k + i
                    got = wide[c, pl.ds(base + q, frames, stride=padded), :]
                    rows.append(got if real == sent else jnp.where(q < real, got, 0.0))
                both = jnp.concatenate(rows, axis=0).astype(bf16)
                out[place, c * 128 : (c + 1) * 128] = both

        pl.loop(0, sent // 2)(two)


def pack(tm_count, patches_dev, offset, real, sent, tokens, grads):
    _, frames, patches, width = tokens.shape
    joined = grads.shape[3]
    padded = round_up(max(patches, tm_count * patches_dev) + 2, 8)
    return pl.pallas_call(
        functools.partial(pack_kernel, tm_count, patches_dev, offset, real, sent, padded),
        out_shape=[jax.ShapeDtypeStruct((sent * frames, width + joined), bf16)] * tm_count,
        in_specs=[pl.BlockSpec(memory_space=pltpu.VMEM)] * 2,
        out_specs=[pl.BlockSpec(memory_space=pltpu.VMEM)] * tm_count,
        scratch_shapes=[pltpu.VMEM(((width + joined) // 128, frames * padded, 128), f32)],
        compiler_params=pltpu.CompilerParams(vmem_limit_bytes=vmem_limit),
        cost_estimate=pl.CostEstimate(flops=0, bytes_accessed=8_000_000, transcendentals=0),
    )(tokens, grads)


def unpack_kernel(tm_count, patches_dev, chunks, padded, joined, *refs):
    count = tm_count * len(chunks)
    ins = refs[:count]
    mixed_ref, grad_ref, wide = refs[count:]
    frames, patches = mixed_ref.shape[1:3]
    me = lax.axis_index("tm")

    def spread(place, values):
        for c in range(wide.shape[0]):
            wide[c, pl.ds(place, frames, stride=padded), :] = values[:, c * 128 : (c + 1) * 128]

    offset = 0
    for c, (real, sent) in enumerate(chunks):
        for r in range(tm_count):
            source = ins[c * tm_count + r]
            base = (me ^ r) * patches_dev + offset

            def two(k, base=base, source=source):
                both = source[
                    pl.ds(pl.multiple_of(k * 2 * frames, 2 * frames), 2 * frames), :
                ].astype(f32)
                for i in range(2):
                    spread(base + 2 * k + i, both[i * frames : (i + 1) * frames])

            pl.loop(0, real // 2)(two)
            if real % 2:
                k = real // 2
                both = source[k * 2 * frames : (k + 1) * 2 * frames, :].astype(f32)
                spread(base + real - 1, both[:frames])
        offset += real
    for f in range(frames):
        rows = slice(f * padded, f * padded + patches)
        for c in range(wide.shape[0]):
            at = c * 128
            ref, at = (mixed_ref, at) if at < joined else (grad_ref, at - joined)
            ref[0, f, :, at : at + 128] = wide[c, rows].astype(bf16)


def unpack(tm_count, patches_dev, chunks, frames, patches, joined, width, pieces):
    padded = round_up(max(patches, tm_count * patches_dev) + 2, 8)
    return pl.pallas_call(
        functools.partial(unpack_kernel, tm_count, patches_dev, chunks, padded, joined),
        out_shape=[
            jax.ShapeDtypeStruct((1, frames, patches, joined), bf16),
            jax.ShapeDtypeStruct((1, frames, patches, width), bf16),
        ],
        in_specs=[pl.BlockSpec(memory_space=pltpu.VMEM)] * len(pieces),
        out_specs=[pl.BlockSpec(memory_space=pltpu.VMEM)] * 2,
        scratch_shapes=[pltpu.VMEM(((width + joined) // 128, frames * padded, 128), f32)],
        compiler_params=pltpu.CompilerParams(vmem_limit_bytes=vmem_limit),
        cost_estimate=pl.CostEstimate(flops=0, bytes_accessed=12_000_000, transcendentals=0),
    )(*pieces)


def frame_facts(frame, count_ref, starts_ref, kept_ref):
    clip = jnp.zeros_like(frame)
    for b in range(1, starts_ref.shape[1]):
        clip = clip + jnp.where(frame >= b * BLOCK, starts_ref[0, b], 0)
    kept = jnp.zeros_like(frame)
    for g in range(kept_ref.shape[1]):
        kept = jnp.where(frame == g, kept_ref[0, g], kept)
    usable = (frame < count_ref[0]) & (kept == 1)
    return clip, usable


def chunk_kernel(
    tm_count,
    dp_count,
    frames,
    group,
    groups,
    first,
    last,
    count_ref,
    starts_ref,
    kept_ref,
    *rest,
):
    rest = list(rest)
    take = lambda n: [rest.pop(0) for _ in range(n)]
    pieces = take(dp_count)
    sources = take(tm_count)
    before = None if first else take(1)[0]
    outs = take(tm_count)
    sums = take(2) if last else take(1)
    (xs, weight, extra, normed, standard, proj, pgrad, back, acc, ends, allow, sems) = rest
    sent_rows = sources[0].shape[0]
    width = weight.shape[0]
    columns = weight.shape[1]
    joined = columns // 3
    tokens = groups * group * frames * tm_count
    span = group * frames
    shard = width // dp_count
    me = lax.axis_index("tm")
    dp = lax.axis_index("dp")
    z, core = dp // CORES, dp % CORES
    nz = dp_count // CORES

    started = []

    def bring(src, dst):
        copy = pltpu.make_async_copy(src, dst, sems.at[len(started)])
        copy.start()
        started.append(copy)
        return copy

    rows_in = [bring(sources[r], xs.at[r, pl.ds(0, sent_rows)]) for r in range(tm_count)]
    weights_in = []
    for side in range(CORES):
        for k in range(nz):
            owner = lax.rem(z + nz - k, nz) * CORES + (core ^ side)
            piece = pieces[side * nz + k]
            place = pl.ds(pl.multiple_of(owner * shard, shard), shard)
            weights_in.append(bring(piece.at[pl.ds(0, shard)], weight.at[place]))
            weights_in.append(
                bring(piece.at[pl.ds(shard, EXTRA)], extra.at[side * nz + k])
            )
    if not first:
        acc_in = bring(before, acc)
    if xs.shape[1] > sent_rows:
        for r in range(tm_count):
            xs[r, sent_rows:, :] = jnp.zeros((xs.shape[1] - sent_rows, columns), bf16)

    row = lax.broadcasted_iota(jnp.int32, (tm_count * frames, tokens // groups), 0)
    lane = lax.broadcasted_iota(jnp.int32, (tm_count * frames, tokens // groups), 1)
    key_frame = (me ^ (row // frames)) * frames + row % frames
    query_frame = (me ^ (lane // span)) * frames + lane % frames
    key_clip, key_usable = frame_facts(key_frame, count_ref, starts_ref, kept_ref)
    query_clip, _ = frame_facts(query_frame, count_ref, starts_ref, kept_ref)
    ok = (key_clip == query_clip) & (key_usable | (key_frame == query_frame))
    allow[...] = jnp.where(ok, 1.0, 0.0)
    token = lax.broadcasted_iota(jnp.int32, (tokens // groups, 128), 0)
    token_frame = (me ^ (token // span)) * frames + token % frames
    token_valid = token_frame < count_ref[0]

    for copy in weights_in:
        copy.wait()
    gain = functools.reduce(
        lambda a, b: a + b, [extra[i, 0:1, :width].astype(f32) for i in range(dp_count)]
    )
    bias = functools.reduce(
        lambda a, b: a + b, [extra[i, 1:2, :width].astype(f32) for i in range(dp_count)]
    )
    for copy in rows_in:
        copy.wait()

    unit = tokens // groups

    @pl.loop(0, groups)
    def _(j):
        rows = pl.ds(pl.multiple_of(j * span, span), span)
        x = jnp.concatenate([xs[r, rows, :width] for r in range(tm_count)], axis=0).astype(f32)
        centred = x - jnp.mean(x, axis=-1, keepdims=True)
        inverse = lax.rsqrt(jnp.mean(centred * centred, axis=-1, keepdims=True) + epsilon)
        std = centred * inverse
        at = pl.ds(pl.multiple_of(j * unit, unit), unit)
        standard[at, :] = std
        ends[at, :] = jnp.broadcast_to(inverse, (unit, 128))
        normed[at, :] = (std * gain + bias).astype(bf16)

    for part in range(3):
        cut = slice(part * joined, (part + 1) * joined)
        proj[:, cut] = jnp.dot(
            normed[...], weight[:, cut], preferred_element_type=f32
        ).astype(bf16)

    pairs = joined // 128
    wide = joined // HEADS
    scale = wide ** (-0.5)
    low = lax.broadcasted_iota(jnp.int32, (unit, 128), 1) < wide
    patch_lane = (lax.broadcasted_iota(jnp.int32, (1, unit), 1) // frames) % group

    def stack(block):
        zero = jnp.zeros_like(block)
        return jnp.concatenate(
            [jnp.where(low, block, zero), jnp.where(low, zero, block)], axis=0
        )

    def compact(full):
        parts = full.reshape(2, tm_count, group, frames, unit)
        got = parts[:, :, 0]
        for p in range(1, group):
            got = jnp.where(patch_lane == p, parts[:, :, p], got)
        return got.reshape(2, tm_count * frames, unit)

    def expand(small):
        small = small.reshape(2, tm_count, 1, frames, unit)
        pieces = [jnp.where(patch_lane == p, small, 0.0) for p in range(group)]
        return jnp.concatenate(pieces, axis=2).reshape(2 * unit, unit).astype(bf16)

    nt = (((1,), (1,)), ((), ()))
    tn = (((0,), (0,)), ((), ()))

    @pl.loop(0, groups)
    def _(j):
        rows = pl.ds(pl.multiple_of(j * span, span), span)
        at = pl.ds(pl.multiple_of(j * unit, unit), unit)
        allowed = allow[...] > 0.5
        for pair in range(pairs):
            col = slice(pair * 128, (pair + 1) * 128)
            q2 = proj[at, pair * 128 : (pair + 1) * 128]
            k2 = proj[at, joined + pair * 128 : joined + (pair + 1) * 128]
            v2 = proj[at, 2 * joined + pair * 128 : 2 * joined + (pair + 1) * 128]
            up = jnp.concatenate(
                [
                    xs[r, rows, width + pair * 128 : width + (pair + 1) * 128]
                    for r in range(tm_count)
                ],
                axis=0,
            )
            up = jnp.where(token_valid, up, jnp.zeros_like(up))
            kcat, vcat, qcat, ucat = stack(k2), stack(v2), stack(q2), stack(up)
            scores = compact(lax.dot_general(kcat, q2, nt, preferred_element_type=f32))
            scores = jnp.where(allowed, scores * scale, masked_value)
            shifted = jnp.exp(scores - jnp.max(scores, axis=1, keepdims=True))
            probs = shifted / jnp.sum(shifted, axis=1, keepdims=True)
            full = expand(probs)
            mixed = lax.dot_general(full, vcat, tn, preferred_element_type=f32)
            mixed = jnp.where(token_valid, mixed, 0.0).astype(bf16)
            across = jnp.concatenate([full[:unit], full[unit:]], axis=1)
            value_grad = jnp.dot(across, ucat, preferred_element_type=f32)
            wgrad = compact(lax.dot_general(vcat, up, nt, preferred_element_type=f32))
            inner = jnp.sum(wgrad * probs, axis=1, keepdims=True)
            sgrad = expand(probs * (wgrad - inner) * scale)
            query_grad = lax.dot_general(sgrad, kcat, tn, preferred_element_type=f32)
            sacross = jnp.concatenate([sgrad[:unit], sgrad[unit:]], axis=1)
            key_grad = jnp.dot(sacross, qcat, preferred_element_type=f32)
            for r in range(tm_count):
                back[r, rows, col] = mixed[r * span : (r + 1) * span]
            pgrad[at, pair * 128 : (pair + 1) * 128] = query_grad.astype(bf16)
            pgrad[at, joined + pair * 128 : joined + (pair + 1) * 128] = key_grad.astype(bf16)
            pgrad[at, 2 * joined + pair * 128 : 2 * joined + (pair + 1) * 128] = (
                value_grad.astype(bf16)
            )

    if not first:
        acc_in.wait()
    for part in range(3):
        cut = slice(part * joined, (part + 1) * joined)
        share = lax.dot_general(normed[...], pgrad[:, cut], tn, preferred_element_type=f32)
        if first:
            acc[:width, cut] = share
        else:
            acc[:width, cut] += share

    if first:
        acc[width:, :] = jnp.zeros((acc.shape[0] - width, columns), f32)

    @pl.loop(0, groups)
    def _(j):
        rows = pl.ds(pl.multiple_of(j * span, span), span)
        at = pl.ds(pl.multiple_of(j * unit, unit), unit)
        ngrad = lax.dot_general(
            pgrad[at, :], weight[...], nt, preferred_element_type=f32
        )
        ngrad = ngrad.astype(bf16).astype(f32)
        std = standard[at, :]
        product = ngrad * std
        acc[width : width + 8, :width] += jnp.sum(product.reshape(unit // 8, 8, width), axis=0)
        acc[width + 8 : width + 16, :width] += jnp.sum(
            ngrad.reshape(unit // 8, 8, width), axis=0
        )
        scaled = ngrad * gain
        grad = ends[at, 0:1] * (
            scaled
            - jnp.mean(scaled, axis=-1, keepdims=True)
            - std * jnp.mean(product * gain, axis=-1, keepdims=True)
        )
        grad = grad.astype(bf16)
        for r in range(tm_count):
            back[r, rows, joined:] = grad[r * span : (r + 1) * span]

    gone = [bring(back.at[r, pl.ds(0, sent_rows)], outs[r]) for r in range(tm_count)]
    if not last:
        gone.append(bring(acc, sums[0]))
    else:
        keep, send = sums
        extra_rows = jnp.concatenate(
            [
                jnp.sum(acc[width : width + 8, :], axis=0, keepdims=True),
                jnp.sum(acc[width + 8 : width + 16, :], axis=0, keepdims=True),
                jnp.zeros((EXTRA - 2, columns), f32),
            ],
            axis=0,
        ).astype(bf16)
        for k in range(nz):
            owner = lax.rem(z + k, nz) * CORES
            for ref, side in ((keep, core), (send, 1 - core)):
                place = pl.ds(pl.multiple_of((owner + side) * shard, shard), shard)
                ref[k, :shard, :] = acc[place, :].astype(bf16)
                ref[k, shard:, :] = extra_rows
    for copy in gone:
        copy.wait()


def chunk(tm_count, dp_count, frames, group, first, last, facts, pieces, sources, before):
    sent_rows, total = sources[0].shape
    shard, columns = pieces[0].shape[0] - EXTRA, pieces[0].shape[1]
    width = shard * dp_count
    span = group * frames
    groups = -(-sent_rows // span)
    tokens = groups * span * tm_count
    nz = dp_count // CORES
    outs = [jax.ShapeDtypeStruct((sent_rows, total), bf16)] * tm_count
    anywhere = pl.BlockSpec(memory_space=pl.ANY)
    out_specs = [anywhere] * tm_count
    if last:
        outs += [jax.ShapeDtypeStruct((nz, shard + EXTRA, columns), bf16)] * 2
        out_specs += [pl.BlockSpec(memory_space=pltpu.VMEM)] * 2
    else:
        outs += [jax.ShapeDtypeStruct((width + 16, columns), f32)]
        out_specs += [anywhere]
    args = list(facts) + list(pieces) + list(sources) + ([] if first else [before])
    scratch = [
        pltpu.VMEM((tm_count, groups * span, total), bf16),
        pltpu.VMEM((width, columns), bf16),
        pltpu.VMEM((dp_count, EXTRA, columns), bf16),
        pltpu.VMEM((tokens, width), bf16),
        pltpu.VMEM((tokens, width), f32),
        pltpu.VMEM((tokens, columns), bf16),
        pltpu.VMEM((tokens, columns), bf16),
        pltpu.VMEM((tm_count, groups * span, total), bf16),
        pltpu.VMEM((width + 16, columns), f32),
        pltpu.VMEM((tokens, 128), f32),
        pltpu.VMEM((tm_count * frames, tokens // groups), f32),
        pltpu.SemaphoreType.DMA((2 * tm_count + 2 * dp_count + 2,)),
    ]
    return pl.pallas_call(
        functools.partial(
            chunk_kernel, tm_count, dp_count, frames, group, groups, first, last
        ),
        out_shape=outs,
        in_specs=[pl.BlockSpec(memory_space=pltpu.SMEM)] * 3 + [anywhere] * (len(args) - 3),
        out_specs=out_specs,
        scratch_shapes=scratch,
        compiler_params=pltpu.CompilerParams(vmem_limit_bytes=vmem_limit),
        cost_estimate=pl.CostEstimate(
            flops=6 * tokens * width * columns, bytes_accessed=10_000_000, transcendentals=0
        ),
    )(*args)


def partner(count, r):
    return [(i, i ^ r) for i in range(count)]


def body(
    video_tokens,
    norm_gain,
    norm_bias,
    qkv_weight,
    frame_counts,
    clip_starts,
    frame_kept,
    attended_grad,
):
    tm_count, dp_count = lax.axis_size("tm"), lax.axis_size("dp")
    nz = dp_count // CORES
    _, frames, patches, width = video_tokens.shape
    joined = attended_grad.shape[3]
    shard, columns = qkv_weight.shape
    patches_dev = -(-patches // tm_count)
    group = max(2, 128 // (frames * tm_count))
    chunks = chunk_sizes(patches_dev, group, 2)
    dp = lax.axis_index("dp")

    def swap(array, r):
        return lax.ppermute(array, "tm", partner(tm_count, r))

    packed, offset = [], 0
    for real, sent in chunks:
        packed.append(
            pack(tm_count, patches_dev, offset, real, sent, video_tokens, attended_grad)
        )
        offset += real
    gathered = [
        [part if r == 0 else swap(part, r) for r, part in enumerate(blocks)]
        for blocks in packed
    ]

    lines = jnp.zeros((EXTRA, columns), bf16)
    lines = lax.dynamic_update_slice(lines, norm_gain[None], (0, dp * shard))
    lines = lax.dynamic_update_slice(lines, norm_bias[None], (1, dp * shard))
    own = jnp.concatenate([qkv_weight, lines], axis=0)
    along = [own] + [
        lax.ppermute(own, "dp", [(i, (i + CORES * k) % dp_count) for i in range(dp_count)])
        for k in range(1, nz)
    ]
    pieces = along + [lax.ppermute(a, "dp", partner(dp_count, 1)) for a in along]

    facts = (frame_counts, clip_starts, frame_kept)
    results, total = [], None
    for c, sources in enumerate(gathered):
        first, last = c == 0, c == len(chunks) - 1
        got = chunk(
            tm_count, dp_count, frames, group, first, last, facts, pieces, sources, total
        )
        results.append([part if r == 0 else swap(part, r) for r, part in enumerate(got[:tm_count])])
        total = got[tm_count]
        sent_half = got[-1]

    other = lax.ppermute(sent_half, "dp", partner(dp_count, 1))
    blocks = [
        lax.optimization_barrier(
            (total[k].astype(f32) + other[k].astype(f32)).astype(bf16)
        )
        for k in range(nz)
    ]
    summed = blocks[0].astype(f32)
    for k in range(1, nz):
        summed = summed + lax.ppermute(
            blocks[k], "dp", [(i, (i + CORES * k) % dp_count) for i in range(dp_count)]
        ).astype(f32)
    r = 1
    while r < tm_count:
        mine = lax.optimization_barrier(summed.astype(bf16))
        summed = mine.astype(f32) + swap(mine, r).astype(f32)
        r *= 2

    attended, tokens_grad = unpack(
        tm_count,
        patches_dev,
        chunks,
        frames,
        patches,
        joined,
        width,
        [part for blocks_out in results for part in blocks_out],
    )
    weight_total = summed[:shard]
    gain_total = lax.dynamic_slice(summed[shard], (dp * shard,), (shard,))
    bias_total = lax.dynamic_slice(summed[shard + 1], (dp * shard,), (shard,))
    return (attended, tokens_grad, weight_total, gain_total, bias_total)


def solution(mesh):
    placed = (
        P("dp", "tm", None, None),
        P("dp"),
        P("dp"),
        P("dp", None),
        P("dp"),
        P("dp", None),
        P("dp", None),
        P("dp", "tm", None, None),
    )
    return jax.shard_map(
        body,
        mesh=mesh,
        in_specs=placed,
        out_specs=(
            P("dp", "tm", None, None),
            P("dp", "tm", None, None),
            P("dp", None),
            P("dp"),
            P("dp"),
        ),
        check_vma=False,
    )
```

```python
import functools

import jax
import jax.numpy as jnp
from jax import lax
from jax.experimental import pallas as pl
from jax.experimental.pallas import tpu as pltpu
from jax.sharding import PartitionSpec as P

HEADS = 6
BLOCK = 16
CORES = 2
EXTRA = 16

masked_value = -1e30
epsilon = 1e-05
vmem_limit = 56 * 1024 * 1024
f32 = jnp.float32
bf16 = jnp.bfloat16


def round_up(value, step):
    return -(-value // step) * step


def chunk_sizes(patches_dev, group, count):
    groups = -(-patches_dev // group)
    count = min(count, groups)
    sizes = []
    left = patches_dev
    for index in range(count - 1):
        taken = (groups // count) * group
        sizes.append(taken)
        left -= taken
    sizes.append(left)
    return sizes


anywhere = pl.BlockSpec(memory_space=pl.ANY)


def run_all(pairs, sems):
    copies = [pltpu.make_async_copy(a, b, sems.at[i]) for i, (a, b) in enumerate(pairs)]
    for copy in copies:
        copy.start()
    return copies


def pack_kernel(tm_count, patches_dev, offset, size, x_ref, grad_ref, *rest):
    outs, sems = rest[:-1], rest[-1]
    width = x_ref.shape[2]
    me = lax.axis_index("tm")
    pairs = []
    for r in range(1, tm_count):
        place = pl.ds((me ^ r) * patches_dev + offset, size)
        pairs.append((x_ref.at[place], outs[r - 1].at[:, :, pl.ds(0, width)]))
        pairs.append(
            (grad_ref.at[place], outs[r - 1].at[:, :, pl.ds(width, grad_ref.shape[2])])
        )
    for copy in run_all(pairs, sems):
        copy.wait()


def pack(tm_count, patches_dev, offset, size, tokens, grads):
    _, frames, width = tokens.shape
    total = width + grads.shape[2]
    return pl.pallas_call(
        functools.partial(pack_kernel, tm_count, patches_dev, offset, size),
        out_shape=[jax.ShapeDtypeStruct((size, frames, total), bf16)] * (tm_count - 1),
        in_specs=[anywhere] * 2,
        out_specs=[pl.BlockSpec(memory_space=pltpu.VMEM)] * (tm_count - 1),
        scratch_shapes=[pltpu.SemaphoreType.DMA((2 * tm_count,))],
        compiler_params=pltpu.CompilerParams(vmem_limit_bytes=vmem_limit),
    )(tokens, grads)


def unpack_kernel(tm_count, patches_dev, offset, size, *refs):
    ins = refs[2 : tm_count + 1]
    mixed_ref, grad_ref, held, sems, out_sems = refs[tm_count + 1 :]
    joined, width = mixed_ref.shape[2], grad_ref.shape[2]
    me = lax.axis_index("tm")
    arriving = run_all([(ins[r - 1], held.at[r - 1]) for r in range(1, tm_count)], sems)
    leaving = []
    for r in range(1, tm_count):
        place = pl.ds((me ^ r) * patches_dev + offset, size)
        arriving[r - 1].wait()
        for at, ref in ((0, mixed_ref), (joined, grad_ref)):
            copy = pltpu.make_async_copy(
                held.at[r - 1, :, :, pl.ds(at, ref.shape[2])],
                ref.at[place],
                out_sems.at[len(leaving)],
            )
            copy.start()
            leaving.append(copy)
    for copy in leaving:
        copy.wait()


def unpack(tm_count, patches_dev, offset, size, mixed, grads, blocks):
    return pl.pallas_call(
        functools.partial(unpack_kernel, tm_count, patches_dev, offset, size),
        out_shape=[
            jax.ShapeDtypeStruct(mixed.shape, bf16),
            jax.ShapeDtypeStruct(grads.shape, bf16),
        ],
        in_specs=[anywhere] * (tm_count + 1),
        out_specs=[anywhere] * 2,
        input_output_aliases={0: 0, 1: 1},
        scratch_shapes=[
            pltpu.VMEM((tm_count - 1,) + blocks[0].shape, bf16),
            pltpu.SemaphoreType.DMA((tm_count,)),
            pltpu.SemaphoreType.DMA((2 * tm_count,)),
        ],
        compiler_params=pltpu.CompilerParams(vmem_limit_bytes=vmem_limit),
    )(mixed, grads, *blocks)


def frame_facts(frame, count_ref, starts_ref, kept_ref):
    clip = jnp.zeros_like(frame)
    for b in range(1, starts_ref.shape[1]):
        clip = clip + jnp.where(frame >= b * BLOCK, starts_ref[0, b], 0)
    kept = jnp.zeros_like(frame)
    for g in range(kept_ref.shape[1]):
        kept = jnp.where(frame == g, kept_ref[0, g], kept)
    usable = (frame < count_ref[0]) & (kept == 1)
    return clip, usable


def chunk_kernel(
    tm_count,
    dp_count,
    frames,
    group,
    groups,
    patches_dev,
    offset,
    first,
    last,
    count_ref,
    starts_ref,
    kept_ref,
    *rest,
):
    rest = list(rest)
    take = lambda n: [rest.pop(0) for _ in range(n)]
    pieces = take(dp_count)
    x_ref, grad_ref = take(2)
    sources = take(tm_count - 1)
    if not first:
        before = take(1)[0]
        take(2)
    outs = take(tm_count - 1)
    mixed_ref, tokens_ref = take(2)
    sums = take(2) if last else take(1)
    (xs, weight, extra, normed, standard, proj, pgrad, back, acc, ends, allow, sems) = rest
    size = sources[0].shape[0]
    width = weight.shape[0]
    columns = weight.shape[1]
    joined = columns // 3
    tokens = groups * group * frames * tm_count
    span = group * frames
    shard = width // dp_count
    me = lax.axis_index("tm")
    dp = lax.axis_index("dp")
    z, core = dp // CORES, dp % CORES
    nz = dp_count // CORES

    started = []

    def bring(src, dst):
        copy = pltpu.make_async_copy(src, dst, sems.at[len(started)])
        copy.start()
        started.append(copy)
        return copy

    mine = pl.ds(me * patches_dev + offset, size)
    kept = pl.ds(0, size)
    rows_in = [
        bring(x_ref.at[mine], xs.at[0, kept, :, pl.ds(0, width)]),
        bring(grad_ref.at[mine], xs.at[0, kept, :, pl.ds(width, joined)]),
    ]
    rows_in += [bring(sources[r - 1], xs.at[r, kept]) for r in range(1, tm_count)]
    weights_in = []
    for side in range(CORES):
        for k in range(nz):
            owner = lax.rem(z + nz - k, nz) * CORES + (core ^ side)
            piece = pieces[side * nz + k]
            place = pl.ds(pl.multiple_of(owner * shard, shard), shard)
            weights_in.append(bring(piece.at[pl.ds(0, shard)], weight.at[place]))
            weights_in.append(
                bring(piece.at[pl.ds(shard, EXTRA)], extra.at[side * nz + k])
            )
    if not first:
        acc_in = bring(before, acc)
    if xs.shape[1] > size:
        for r in range(tm_count):
            xs[r, size:] = jnp.zeros((xs.shape[1] - size,) + xs.shape[2:], bf16)

    row = lax.broadcasted_iota(jnp.int32, (tm_count * frames, tokens // groups), 0)
    lane = lax.broadcasted_iota(jnp.int32, (tm_count * frames, tokens // groups), 1)
    key_frame = (me ^ (row // frames)) * frames + row % frames
    query_frame = (me ^ (lane // span)) * frames + lane % frames
    key_clip, key_usable = frame_facts(key_frame, count_ref, starts_ref, kept_ref)
    query_clip, _ = frame_facts(query_frame, count_ref, starts_ref, kept_ref)
    ok = (key_clip == query_clip) & (key_usable | (key_frame == query_frame))
    allow[...] = jnp.where(ok, 1.0, 0.0)
    token = lax.broadcasted_iota(jnp.int32, (tokens // groups, 128), 0)
    token_frame = (me ^ (token // span)) * frames + token % frames
    token_valid = token_frame < count_ref[0]

    for copy in weights_in:
        copy.wait()
    gain = functools.reduce(
        lambda a, b: a + b, [extra[i, 0:1, :width].astype(f32) for i in range(dp_count)]
    )
    bias = functools.reduce(
        lambda a, b: a + b, [extra[i, 1:2, :width].astype(f32) for i in range(dp_count)]
    )
    for copy in rows_in:
        copy.wait()

    unit = tokens // groups

    def token_rows(j, cut):
        rows = pl.ds(j * group, group)
        return jnp.concatenate(
            [xs[r, rows, :, cut].astype(f32).reshape(span, -1) for r in range(tm_count)], axis=0
        )

    def put_rows(j, cut, values):
        rows = pl.ds(j * group, group)
        for r in range(tm_count):
            block = values[r * span : (r + 1) * span].reshape(group, frames, -1)
            back[r, rows, :, cut] = block.astype(bf16)

    @pl.loop(0, groups)
    def _(j):
        x = token_rows(j, slice(0, width))
        centred = x - jnp.mean(x, axis=-1, keepdims=True)
        inverse = lax.rsqrt(jnp.mean(centred * centred, axis=-1, keepdims=True) + epsilon)
        std = centred * inverse
        at = pl.ds(pl.multiple_of(j * unit, unit), unit)
        standard[at, :] = std
        ends[at, :] = jnp.broadcast_to(inverse, (unit, 128))
        normed[at, :] = (std * gain + bias).astype(bf16)

    for part in range(3):
        cut = slice(part * joined, (part + 1) * joined)
        proj[:, cut] = jnp.dot(
            normed[...], weight[:, cut], preferred_element_type=f32
        ).astype(bf16)

    pairs = joined // 128
    wide = joined // HEADS
    scale = wide ** (-0.5)
    low = lax.broadcasted_iota(jnp.int32, (unit, 128), 1) < wide
    patch_lane = (lax.broadcasted_iota(jnp.int32, (1, unit), 1) // frames) % group

    def stack(block):
        zero = jnp.zeros_like(block)
        return jnp.concatenate(
            [jnp.where(low, block, zero), jnp.where(low, zero, block)], axis=0
        )

    def compact(full):
        parts = full.reshape(2, tm_count, group, frames, unit)
        got = parts[:, :, 0]
        for p in range(1, group):
            got = jnp.where(patch_lane == p, parts[:, :, p], got)
        return got.reshape(2, tm_count * frames, unit)

    def expand(small):
        small = small.reshape(2, tm_count, 1, frames, unit)
        pieces = [jnp.where(patch_lane == p, small, 0.0) for p in range(group)]
        return jnp.concatenate(pieces, axis=2).reshape(2 * unit, unit).astype(bf16)

    nt = (((1,), (1,)), ((), ()))
    tn = (((0,), (0,)), ((), ()))

    @pl.loop(0, groups)
    def _(j):
        at = pl.ds(pl.multiple_of(j * unit, unit), unit)
        allowed = allow[...] > 0.5
        for pair in range(pairs):
            col = slice(pair * 128, (pair + 1) * 128)
            q2 = proj[at, pair * 128 : (pair + 1) * 128]
            k2 = proj[at, joined + pair * 128 : joined + (pair + 1) * 128]
            v2 = proj[at, 2 * joined + pair * 128 : 2 * joined + (pair + 1) * 128]
            up = token_rows(j, slice(width + pair * 128, width + (pair + 1) * 128))
            up = jnp.where(token_valid, up, 0.0).astype(bf16)
            kcat, vcat, qcat, ucat = stack(k2), stack(v2), stack(q2), stack(up)
            scores = compact(lax.dot_general(kcat, q2, nt, preferred_element_type=f32))
            scores = jnp.where(allowed, scores * scale, masked_value)
            shifted = jnp.exp(scores - jnp.max(scores, axis=1, keepdims=True))
            probs = shifted / jnp.sum(shifted, axis=1, keepdims=True)
            full = expand(probs)
            mixed = lax.dot_general(full, vcat, tn, preferred_element_type=f32)
            put_rows(j, col, jnp.where(token_valid, mixed, 0.0))
            across = jnp.concatenate([full[:unit], full[unit:]], axis=1)
            value_grad = jnp.dot(across, ucat, preferred_element_type=f32)
            wgrad = compact(lax.dot_general(vcat, up, nt, preferred_element_type=f32))
            inner = jnp.sum(wgrad * probs, axis=1, keepdims=True)
            sgrad = expand(probs * (wgrad - inner) * scale)
            query_grad = lax.dot_general(sgrad, kcat, tn, preferred_element_type=f32)
            sacross = jnp.concatenate([sgrad[:unit], sgrad[unit:]], axis=1)
            key_grad = jnp.dot(sacross, qcat, preferred_element_type=f32)
            pgrad[at, pair * 128 : (pair + 1) * 128] = query_grad.astype(bf16)
            pgrad[at, joined + pair * 128 : joined + (pair + 1) * 128] = key_grad.astype(bf16)
            pgrad[at, 2 * joined + pair * 128 : 2 * joined + (pair + 1) * 128] = (
                value_grad.astype(bf16)
            )

    if not first:
        acc_in.wait()
    for part in range(3):
        cut = slice(part * joined, (part + 1) * joined)
        share = lax.dot_general(normed[...], pgrad[:, cut], tn, preferred_element_type=f32)
        if first:
            acc[:width, cut] = share
        else:
            acc[:width, cut] += share

    if first:
        acc[width:, :] = jnp.zeros((acc.shape[0] - width, columns), f32)

    @pl.loop(0, groups)
    def _(j):
        at = pl.ds(pl.multiple_of(j * unit, unit), unit)
        ngrad = lax.dot_general(
            pgrad[at, :], weight[...], nt, preferred_element_type=f32
        )
        ngrad = ngrad.astype(bf16).astype(f32)
        std = standard[at, :]
        product = ngrad * std
        acc[width : width + 8, :width] += jnp.sum(product.reshape(unit // 8, 8, width), axis=0)
        acc[width + 8 : width + 16, :width] += jnp.sum(
            ngrad.reshape(unit // 8, 8, width), axis=0
        )
        scaled = ngrad * gain
        grad = ends[at, 0:1] * (
            scaled
            - jnp.mean(scaled, axis=-1, keepdims=True)
            - std * jnp.mean(product * gain, axis=-1, keepdims=True)
        )
        put_rows(j, slice(joined, columns), grad)

    gone = [bring(back.at[r, kept], outs[r - 1]) for r in range(1, tm_count)]
    gone.append(bring(back.at[0, kept, :, pl.ds(0, joined)], mixed_ref.at[mine]))
    gone.append(bring(back.at[0, kept, :, pl.ds(joined, width)], tokens_ref.at[mine]))
    if not last:
        gone.append(bring(acc, sums[0]))
    else:
        keep, send = sums
        extra_rows = jnp.concatenate(
            [
                jnp.sum(acc[width : width + 8, :], axis=0, keepdims=True),
                jnp.sum(acc[width + 8 : width + 16, :], axis=0, keepdims=True),
                jnp.zeros((EXTRA - 2, columns), f32),
            ],
            axis=0,
        ).astype(bf16)
        for k in range(nz):
            owner = lax.rem(z + k, nz) * CORES
            for ref, side in ((keep, core), (send, 1 - core)):
                place = pl.ds(pl.multiple_of((owner + side) * shard, shard), shard)
                ref[k, :shard, :] = acc[place, :].astype(bf16)
                ref[k, shard:, :] = extra_rows
    for copy in gone:
        copy.wait()


def chunk(
    tm_count, dp_count, group, patches_dev, offset, first, last, facts, pieces, sources, before
):
    tokens_in, grads_in, blocks = sources
    size, frames, total = blocks[0].shape
    shard, columns = pieces[0].shape[0] - EXTRA, pieces[0].shape[1]
    width = shard * dp_count
    groups = -(-size // group)
    tokens = groups * group * frames * tm_count
    nz = dp_count // CORES
    outs = [jax.ShapeDtypeStruct((size, frames, total), bf16)] * (tm_count - 1)
    outs += [
        jax.ShapeDtypeStruct(grads_in.shape, bf16),
        jax.ShapeDtypeStruct(tokens_in.shape, bf16),
    ]
    out_specs = [anywhere] * len(outs)
    if last:
        outs += [jax.ShapeDtypeStruct((nz, shard + EXTRA, columns), bf16)] * 2
        out_specs += [pl.BlockSpec(memory_space=pltpu.VMEM)] * 2
    else:
        outs += [jax.ShapeDtypeStruct((width + 16, columns), f32)]
        out_specs += [anywhere]
    args = list(facts) + list(pieces) + [tokens_in, grads_in] + list(blocks)
    aliases = {}
    if not first:
        args += list(before)
        aliases = {len(args) - 2: tm_count - 1, len(args) - 1: tm_count}
    rows = (tm_count, groups * group, frames, total)
    scratch = [
        pltpu.VMEM(rows, bf16),
        pltpu.VMEM((width, columns), bf16),
        pltpu.VMEM((dp_count, EXTRA, columns), bf16),
        pltpu.VMEM((tokens, width), bf16),
        pltpu.VMEM((tokens, width), f32),
        pltpu.VMEM((tokens, columns), bf16),
        pltpu.VMEM((tokens, columns), bf16),
        pltpu.VMEM(rows, bf16),
        pltpu.VMEM((width + 16, columns), f32),
        pltpu.VMEM((tokens, 128), f32),
        pltpu.VMEM((tm_count * frames, tokens // groups), f32),
        pltpu.SemaphoreType.DMA((2 * tm_count + 2 * dp_count + 8,)),
    ]
    return pl.pallas_call(
        functools.partial(
            chunk_kernel,
            tm_count,
            dp_count,
            frames,
            group,
            groups,
            patches_dev,
            offset,
            first,
            last,
        ),
        out_shape=outs,
        in_specs=[pl.BlockSpec(memory_space=pltpu.SMEM)] * 3 + [anywhere] * (len(args) - 3),
        out_specs=out_specs,
        scratch_shapes=scratch,
        input_output_aliases=aliases,
        compiler_params=pltpu.CompilerParams(vmem_limit_bytes=vmem_limit),
    )(*args)


def partner(count, r):
    return [(i, i ^ r) for i in range(count)]


def body(
    video_tokens,
    norm_gain,
    norm_bias,
    qkv_weight,
    frame_counts,
    clip_starts,
    frame_kept,
    attended_grad,
):
    tm_count, dp_count = lax.axis_size("tm"), lax.axis_size("dp")
    nz = dp_count // CORES
    _, frames, patches, width = video_tokens.shape
    joined = attended_grad.shape[3]
    shard, columns = qkv_weight.shape
    patches_dev = -(-patches // tm_count)
    group = max(2, 128 // (frames * tm_count))
    chunks = chunk_sizes(patches_dev, group, 2)
    dp = lax.axis_index("dp")

    def swap(array, r):
        return lax.ppermute(array, "tm", partner(tm_count, r))

    spare = ((0, tm_count * patches_dev - patches), (0, 0), (0, 0))
    tokens = jnp.pad(video_tokens[0].transpose(1, 0, 2), spare)
    upstream = jnp.pad(attended_grad[0].transpose(1, 0, 2), spare)
    offsets = [sum(chunks[:c]) for c in range(len(chunks))]
    gathered = []
    for offset, size in zip(offsets, chunks):
        blocks = pack(tm_count, patches_dev, offset, size, tokens, upstream)
        gathered.append([swap(part, r + 1) for r, part in enumerate(blocks)])

    lines = jnp.zeros((EXTRA, columns), bf16)
    lines = lax.dynamic_update_slice(lines, norm_gain[None], (0, dp * shard))
    lines = lax.dynamic_update_slice(lines, norm_bias[None], (1, dp * shard))
    own = jnp.concatenate([qkv_weight, lines], axis=0)
    along = [own] + [
        lax.ppermute(own, "dp", [(i, (i + CORES * k) % dp_count) for i in range(dp_count)])
        for k in range(1, nz)
    ]
    pieces = along + [lax.ppermute(a, "dp", partner(dp_count, 1)) for a in along]

    facts = (frame_counts, clip_starts, frame_kept)
    results, before = [], None
    for c, blocks in enumerate(gathered):
        first, last = c == 0, c == len(chunks) - 1
        got = chunk(
            tm_count,
            dp_count,
            group,
            patches_dev,
            offsets[c],
            first,
            last,
            facts,
            pieces,
            (tokens, upstream, blocks),
            before,
        )
        results.append([swap(part, r + 1) for r, part in enumerate(got[: tm_count - 1])])
        mixed, grads = got[tm_count - 1 : tm_count + 1]
        before = (got[tm_count + 1], mixed, grads)
    total, sent_half = got[-2:]

    other = lax.ppermute(sent_half, "dp", partner(dp_count, 1))
    blocks = [
        lax.optimization_barrier(
            (total[k].astype(f32) + other[k].astype(f32)).astype(bf16)
        )
        for k in range(nz)
    ]
    summed = blocks[0].astype(f32)
    for k in range(1, nz):
        summed = summed + lax.ppermute(
            blocks[k], "dp", [(i, (i + CORES * k) % dp_count) for i in range(dp_count)]
        ).astype(f32)
    r = 1
    while r < tm_count:
        mine = lax.optimization_barrier(summed.astype(bf16))
        summed = mine.astype(f32) + swap(mine, r).astype(f32)
        r *= 2

    for c, blocks in enumerate(results):
        mixed, grads = unpack(
            tm_count, patches_dev, offsets[c], chunks[c], mixed, grads, blocks
        )
    attended = mixed[:patches].transpose(1, 0, 2)[None]
    tokens_grad = grads[:patches].transpose(1, 0, 2)[None]
    weight_total = summed[:shard]
    gain_total = lax.dynamic_slice(summed[shard], (dp * shard,), (shard,))
    bias_total = lax.dynamic_slice(summed[shard + 1], (dp * shard,), (shard,))
    return (attended, tokens_grad, weight_total, gain_total, bias_total)


def solution(mesh):
    placed = (
        P("dp", "tm", None, None),
        P("dp"),
        P("dp"),
        P("dp", None),
        P("dp"),
        P("dp", None),
        P("dp", None),
        P("dp", "tm", None, None),
    )
    return jax.shard_map(
        body,
        mesh=mesh,
        in_specs=placed,
        out_specs=(
            P("dp", "tm", None, None),
            P("dp", "tm", None, None),
            P("dp", None),
            P("dp"),
            P("dp"),
        ),
        check_vma=False,
    )
```

```python
import functools

import jax
import jax.numpy as jnp
from jax import lax
from jax.experimental import pallas as pl
from jax.experimental.pallas import tpu as pltpu
from jax.sharding import PartitionSpec as P

HEADS = 6
BLOCK = 16
CORES = 2
EXTRA = 16

masked_value = -1e30
epsilon = 1e-05
vmem_limit = 56 * 1024 * 1024
f32 = jnp.float32
bf16 = jnp.bfloat16


def round_up(value, step):
    return -(-value // step) * step


def chunk_sizes(patches_dev, group, count):
    groups = -(-patches_dev // group)
    count = min(count, groups)
    sizes = []
    left = patches_dev
    for index in range(count - 1):
        taken = (groups // count) * group
        sizes.append(taken)
        left -= taken
    sizes.append(left)
    return sizes


anywhere = pl.BlockSpec(memory_space=pl.ANY)


def run_all(pairs, sems):
    copies = [pltpu.make_async_copy(a, b, sems.at[i]) for i, (a, b) in enumerate(pairs)]
    for copy in copies:
        copy.start()
    return copies


def pack_kernel(tm_count, patches_dev, offset, size, x_ref, grad_ref, *rest):
    sems = rest[-1]
    outs = rest[-tm_count:-1]
    width = x_ref.shape[2]
    me = lax.axis_index("tm")
    pairs = []
    for r in range(1, tm_count):
        place = pl.ds((me ^ r) * patches_dev + offset, size)
        pairs.append((x_ref.at[place], outs[r - 1].at[:, :, pl.ds(0, width)]))
        pairs.append(
            (grad_ref.at[place], outs[r - 1].at[:, :, pl.ds(width, grad_ref.shape[2])])
        )
    if len(rest) > tm_count:
        weight_ref, lines_ref, own_ref = rest[:3]
        shard, columns = weight_ref.shape
        pairs.append((weight_ref, own_ref.at[pl.ds(0, shard)]))
    copies = run_all(pairs, sems)
    if len(rest) > tm_count:
        owner = lax.broadcasted_iota(jnp.int32, lines_ref.shape, 1) // shard
        lines = jnp.where(owner == lax.axis_index("dp"), lines_ref[...].astype(f32), 0.0)
        own_ref[shard:, :] = jnp.concatenate(
            [lines, jnp.zeros((EXTRA - lines.shape[0], columns), f32)], axis=0
        ).astype(bf16)
    for copy in copies:
        copy.wait()


def pack(tm_count, patches_dev, offset, size, tokens, grads, weight=None, lines=None):
    _, frames, width = tokens.shape
    total = width + grads.shape[2]
    in_vmem = pl.BlockSpec(memory_space=pltpu.VMEM)
    args, specs = [tokens, grads], [anywhere] * 2
    outs = [jax.ShapeDtypeStruct((size, frames, total), bf16)] * (tm_count - 1)
    if weight is not None:
        args += [weight, lines]
        specs += [anywhere, in_vmem]
        shard, columns = weight.shape
        outs = [jax.ShapeDtypeStruct((shard + EXTRA, columns), bf16)] + outs
    return pl.pallas_call(
        functools.partial(pack_kernel, tm_count, patches_dev, offset, size),
        out_shape=outs,
        in_specs=specs,
        out_specs=[in_vmem] * len(outs),
        scratch_shapes=[pltpu.SemaphoreType.DMA((2 * tm_count,))],
        compiler_params=pltpu.CompilerParams(vmem_limit_bytes=vmem_limit),
    )(*args)


def unpack_kernel(tm_count, patches_dev, offset, size, *refs):
    ins = refs[2 : tm_count + 1]
    mixed_ref, grad_ref, held, sems, out_sems = refs[tm_count + 1 :]
    joined, width = mixed_ref.shape[2], grad_ref.shape[2]
    me = lax.axis_index("tm")
    arriving = run_all([(ins[r - 1], held.at[r - 1]) for r in range(1, tm_count)], sems)
    leaving = []
    for r in range(1, tm_count):
        place = pl.ds((me ^ r) * patches_dev + offset, size)
        arriving[r - 1].wait()
        for at, ref in ((0, mixed_ref), (joined, grad_ref)):
            copy = pltpu.make_async_copy(
                held.at[r - 1, :, :, pl.ds(at, ref.shape[2])],
                ref.at[place],
                out_sems.at[len(leaving)],
            )
            copy.start()
            leaving.append(copy)
    for copy in leaving:
        copy.wait()


def unpack(tm_count, patches_dev, offset, size, mixed, grads, blocks):
    return pl.pallas_call(
        functools.partial(unpack_kernel, tm_count, patches_dev, offset, size),
        out_shape=[
            jax.ShapeDtypeStruct(mixed.shape, bf16),
            jax.ShapeDtypeStruct(grads.shape, bf16),
        ],
        in_specs=[anywhere] * (tm_count + 1),
        out_specs=[anywhere] * 2,
        input_output_aliases={0: 0, 1: 1},
        scratch_shapes=[
            pltpu.VMEM((tm_count - 1,) + blocks[0].shape, bf16),
            pltpu.SemaphoreType.DMA((tm_count,)),
            pltpu.SemaphoreType.DMA((2 * tm_count,)),
        ],
        compiler_params=pltpu.CompilerParams(vmem_limit_bytes=vmem_limit),
    )(mixed, grads, *blocks)


def frame_facts(frame, count_ref, starts_ref, kept_ref):
    clip = jnp.zeros_like(frame)
    for b in range(1, starts_ref.shape[1]):
        clip = clip + jnp.where(frame >= b * BLOCK, starts_ref[0, b], 0)
    kept = jnp.zeros_like(frame)
    for g in range(kept_ref.shape[1]):
        kept = jnp.where(frame == g, kept_ref[0, g], kept)
    usable = (frame < count_ref[0]) & (kept == 1)
    return clip, usable


def chunk_kernel(
    tm_count,
    dp_count,
    frames,
    group,
    groups,
    patches_dev,
    offset,
    first,
    last,
    count_ref,
    starts_ref,
    kept_ref,
    *rest,
):
    nz = dp_count // CORES
    rest = list(rest)
    take = lambda n: [rest.pop(0) for _ in range(n)]
    pieces = take(nz + 1)
    x_ref, grad_ref = take(2)
    sources = take(tm_count - 1)
    if not first:
        before, before_ends = take(2)
        take(2)
    outs = take(tm_count - 1)
    mixed_ref, tokens_ref = take(2)
    sums = take(4) if last else take(2)
    (xs, weight, extra, normed, standard, proj, pgrad, back, acc, ends, tails, allow, sems) = rest
    size = sources[0].shape[0]
    width = weight.shape[0]
    columns = weight.shape[1]
    joined = columns // 3
    tokens = groups * group * frames * tm_count
    span = group * frames
    shard = width // dp_count
    me = lax.axis_index("tm")
    dp = lax.axis_index("dp")
    z, core = dp // CORES, dp % CORES

    started = []

    def bring(src, dst):
        copy = pltpu.make_async_copy(src, dst, sems.at[len(started)])
        copy.start()
        started.append(copy)
        return copy

    mine = pl.ds(me * patches_dev + offset, size)
    kept = pl.ds(0, size)
    rows_in = [
        bring(x_ref.at[mine], xs.at[0, kept, :, pl.ds(0, width)]),
        bring(grad_ref.at[mine], xs.at[0, kept, :, pl.ds(width, joined)]),
    ]
    rows_in += [bring(sources[r - 1], xs.at[r, kept]) for r in range(1, tm_count)]
    weights_in = []
    for side in range(CORES):
        for k in range(nz):
            owner = lax.rem(z + nz - k, nz) * CORES + (core ^ side)
            piece = pieces[k] if side == 0 else pieces[nz].at[k]
            place = pl.ds(pl.multiple_of(owner * shard, shard), shard)
            weights_in.append(bring(piece.at[pl.ds(0, shard)], weight.at[place]))
            weights_in.append(
                bring(piece.at[pl.ds(shard, EXTRA)], extra.at[side * nz + k])
            )
    if not first:
        acc_in = [bring(before, acc), bring(before_ends, tails)]
    if xs.shape[1] > size:
        for r in range(tm_count):
            xs[r, size:] = jnp.zeros((xs.shape[1] - size,) + xs.shape[2:], bf16)

    row = lax.broadcasted_iota(jnp.int32, (tm_count * frames, tokens // groups), 0)
    lane = lax.broadcasted_iota(jnp.int32, (tm_count * frames, tokens // groups), 1)
    key_frame = (me ^ (row // frames)) * frames + row % frames
    query_frame = (me ^ (lane // span)) * frames + lane % frames
    key_clip, key_usable = frame_facts(key_frame, count_ref, starts_ref, kept_ref)
    query_clip, _ = frame_facts(query_frame, count_ref, starts_ref, kept_ref)
    ok = (key_clip == query_clip) & (key_usable | (key_frame == query_frame))
    allow[...] = jnp.where(ok, 1.0, 0.0)
    token = lax.broadcasted_iota(jnp.int32, (tokens // groups, 128), 0)
    token_frame = (me ^ (token // span)) * frames + token % frames
    token_valid = token_frame < count_ref[0]

    for copy in weights_in:
        copy.wait()
    gain = functools.reduce(
        lambda a, b: a + b, [extra[i, 0:1, :width].astype(f32) for i in range(dp_count)]
    )
    bias = functools.reduce(
        lambda a, b: a + b, [extra[i, 1:2, :width].astype(f32) for i in range(dp_count)]
    )
    for copy in rows_in:
        copy.wait()

    unit = tokens // groups

    def token_rows(j, cut):
        rows = pl.ds(j * group, group)
        return jnp.concatenate(
            [xs[r, rows, :, cut].astype(f32).reshape(span, -1) for r in range(tm_count)], axis=0
        )

    def put_rows(j, cut, values):
        rows = pl.ds(j * group, group)
        for r in range(tm_count):
            block = values[r * span : (r + 1) * span].reshape(group, frames, -1)
            back[r, rows, :, cut] = block.astype(bf16)

    @pl.loop(0, groups)
    def _(j):
        x = token_rows(j, slice(0, width))
        centred = x - jnp.mean(x, axis=-1, keepdims=True)
        inverse = lax.rsqrt(jnp.mean(centred * centred, axis=-1, keepdims=True) + epsilon)
        std = centred * inverse
        at = pl.ds(pl.multiple_of(j * unit, unit), unit)
        standard[at, :] = std
        ends[at, :] = jnp.broadcast_to(inverse, (unit, 128))
        normed[at, :] = (std * gain + bias).astype(bf16)

    for part in range(3):
        cut = slice(part * joined, (part + 1) * joined)
        proj[:, cut] = jnp.dot(
            normed[...], weight[:, cut], preferred_element_type=f32
        ).astype(bf16)

    pairs = joined // 128
    wide = joined // HEADS
    scale = wide ** (-0.5)
    low = lax.broadcasted_iota(jnp.int32, (unit, 128), 1) < wide
    patch_lane = (lax.broadcasted_iota(jnp.int32, (1, unit), 1) // frames) % group

    def stack(block):
        zero = jnp.zeros_like(block)
        return jnp.concatenate(
            [jnp.where(low, block, zero), jnp.where(low, zero, block)], axis=0
        )

    def compact(full):
        parts = full.reshape(2, tm_count, group, frames, unit)
        got = parts[:, :, 0]
        for p in range(1, group):
            got = jnp.where(patch_lane == p, parts[:, :, p], got)
        return got.reshape(2, tm_count * frames, unit)

    def expand(small):
        small = small.reshape(2, tm_count, 1, frames, unit)
        pieces = [jnp.where(patch_lane == p, small, 0.0) for p in range(group)]
        return jnp.concatenate(pieces, axis=2).reshape(2 * unit, unit).astype(bf16)

    nt = (((1,), (1,)), ((), ()))
    tn = (((0,), (0,)), ((), ()))

    @pl.loop(0, groups)
    def _(j):
        at = pl.ds(pl.multiple_of(j * unit, unit), unit)
        allowed = allow[...] > 0.5
        every = range(pairs)
        cols = [slice(pair * 128, (pair + 1) * 128) for pair in every]
        cut = lambda part: [
            proj[at, part * joined + pair * 128 : part * joined + (pair + 1) * 128]
            for pair in every
        ]
        q2, k2, v2 = cut(0), cut(1), cut(2)
        up = [
            token_rows(j, slice(width + pair * 128, width + (pair + 1) * 128)) for pair in every
        ]
        up = [jnp.where(token_valid, u, 0.0).astype(bf16) for u in up]
        kcat, vcat = [stack(k) for k in k2], [stack(v) for v in v2]
        scores = [
            compact(lax.dot_general(kcat[i], q2[i], nt, preferred_element_type=f32))
            for i in every
        ]
        wgrad = [
            compact(lax.dot_general(vcat[i], up[i], nt, preferred_element_type=f32))
            for i in every
        ]
        probs = []
        for i in every:
            masked = jnp.where(allowed, scores[i] * scale, masked_value)
            shifted = jnp.exp(masked - jnp.max(masked, axis=1, keepdims=True))
            probs.append(shifted * (1.0 / jnp.sum(shifted, axis=1, keepdims=True)))
        full = [expand(p) for p in probs]
        sgrad = []
        for i in every:
            inner = jnp.sum(wgrad[i] * probs[i], axis=1, keepdims=True)
            sgrad.append(expand(probs[i] * (wgrad[i] - inner) * scale))
        for i in every:
            mixed = lax.dot_general(full[i], vcat[i], tn, preferred_element_type=f32)
            put_rows(j, cols[i], jnp.where(token_valid, mixed, 0.0))
            across = jnp.concatenate([full[i][:unit], full[i][unit:]], axis=1)
            value_grad = jnp.dot(across, stack(up[i]), preferred_element_type=f32)
            query_grad = lax.dot_general(sgrad[i], kcat[i], tn, preferred_element_type=f32)
            sacross = jnp.concatenate([sgrad[i][:unit], sgrad[i][unit:]], axis=1)
            key_grad = jnp.dot(sacross, stack(q2[i]), preferred_element_type=f32)
            for part, value in enumerate((query_grad, key_grad, value_grad)):
                place = slice(part * joined + i * 128, part * joined + (i + 1) * 128)
                pgrad[at, place] = value.astype(bf16)

    if not first:
        for copy in acc_in:
            copy.wait()
    else:
        tails[...] = jnp.zeros_like(tails)
    for part in range(3):
        cut = slice(part * joined, (part + 1) * joined)
        share = lax.dot_general(normed[...], pgrad[:, cut], tn, preferred_element_type=f32)
        if first:
            acc[:, cut] = share
        else:
            acc[:, cut] += share

    gone = []
    if not last:
        gone.append(bring(acc, sums[0]))
    normed[...] = lax.dot_general(
        pgrad[...], weight[...], nt, preferred_element_type=f32
    ).astype(bf16)

    @pl.loop(0, groups)
    def _(j):
        at = pl.ds(pl.multiple_of(j * unit, unit), unit)
        ngrad = normed[at, :].astype(f32)
        std = standard[at, :]
        product = ngrad * std
        tails[0:8, :] += jnp.sum(product.reshape(unit // 8, 8, width), axis=0)
        tails[8:16, :] += jnp.sum(ngrad.reshape(unit // 8, 8, width), axis=0)
        scaled = ngrad * gain
        grad = ends[at, 0:1] * (
            scaled
            - jnp.mean(scaled, axis=-1, keepdims=True)
            - std * jnp.mean(product * gain, axis=-1, keepdims=True)
        )
        put_rows(j, slice(joined, columns), grad)

    gone += [bring(back.at[r, kept], outs[r - 1]) for r in range(1, tm_count)]
    gone.append(bring(back.at[0, kept, :, pl.ds(0, joined)], mixed_ref.at[mine]))
    gone.append(bring(back.at[0, kept, :, pl.ds(joined, width)], tokens_ref.at[mine]))
    if not last:
        gone.append(bring(tails, sums[1]))
    else:
        cut = sums[0].shape[1]
        extra_rows = jnp.concatenate(
            [
                jnp.sum(tails[0:8, :], axis=0, keepdims=True),
                jnp.sum(tails[8:16, :], axis=0, keepdims=True),
                jnp.zeros((EXTRA - 2, width), f32),
            ],
            axis=0,
        ).astype(bf16)
        for k in range(nz):
            owner = lax.rem(z + k, nz) * CORES
            for refs, side in ((sums[:2], core), (sums[2:], 1 - core)):
                start = pl.multiple_of((owner + side) * shard, shard)
                refs[0][k] = acc[pl.ds(start, cut), :].astype(bf16)
                refs[1][k, : shard - cut, :] = acc[
                    pl.ds(pl.multiple_of(start + cut, 16), shard - cut), :
                ].astype(bf16)
                refs[1][k, shard - cut :, :width] = extra_rows
                refs[1][k, shard - cut :, width:] = jnp.zeros((EXTRA, columns - width), bf16)
    for copy in gone:
        copy.wait()


def chunk(
    tm_count, dp_count, group, patches_dev, offset, first, last, facts, pieces, sources, before
):
    tokens_in, grads_in, blocks = sources
    size, frames, total = blocks[0].shape
    shard, columns = pieces[0].shape[0] - EXTRA, pieces[0].shape[1]
    width = shard * dp_count
    groups = -(-size // group)
    tokens = groups * group * frames * tm_count
    nz = dp_count // CORES
    outs = [jax.ShapeDtypeStruct((size, frames, total), bf16)] * (tm_count - 1)
    outs += [
        jax.ShapeDtypeStruct(grads_in.shape, bf16),
        jax.ShapeDtypeStruct(tokens_in.shape, bf16),
    ]
    out_specs = [anywhere] * len(outs)
    if last:
        cut = round_up(shard // 2, 16)
        for _ in range(2):
            outs.append(jax.ShapeDtypeStruct((nz, cut, columns), bf16))
            outs.append(jax.ShapeDtypeStruct((nz, shard - cut + EXTRA, columns), bf16))
        out_specs += [pl.BlockSpec(memory_space=pltpu.VMEM)] * 4
    else:
        outs.append(jax.ShapeDtypeStruct((width, columns), f32))
        outs.append(jax.ShapeDtypeStruct((16, width), f32))
        out_specs += [anywhere] * 2
    args = list(facts) + list(pieces) + [tokens_in, grads_in] + list(blocks)
    aliases = {}
    if not first:
        args += list(before)
        aliases = {len(args) - 2: tm_count - 1, len(args) - 1: tm_count}
    rows = (tm_count, groups * group, frames, total)
    scratch = [
        pltpu.VMEM(rows, bf16),
        pltpu.VMEM((width, columns), bf16),
        pltpu.VMEM((dp_count, EXTRA, columns), bf16),
        pltpu.VMEM((tokens, width), bf16),
        pltpu.VMEM((tokens, width), f32),
        pltpu.VMEM((tokens, columns), bf16),
        pltpu.VMEM((tokens, columns), bf16),
        pltpu.VMEM(rows, bf16),
        pltpu.VMEM((width, columns), f32),
        pltpu.VMEM((tokens, 128), f32),
        pltpu.VMEM((16, width), f32),
        pltpu.VMEM((tm_count * frames, tokens // groups), f32),
        pltpu.SemaphoreType.DMA((2 * tm_count + 2 * dp_count + 12,)),
    ]
    return pl.pallas_call(
        functools.partial(
            chunk_kernel,
            tm_count,
            dp_count,
            frames,
            group,
            groups,
            patches_dev,
            offset,
            first,
            last,
        ),
        out_shape=outs,
        in_specs=[pl.BlockSpec(memory_space=pltpu.SMEM)] * 3 + [anywhere] * (len(args) - 3),
        out_specs=out_specs,
        scratch_shapes=scratch,
        input_output_aliases=aliases,
        compiler_params=pltpu.CompilerParams(vmem_limit_bytes=vmem_limit),
    )(*args)


def partner(count, r):
    return [(i, i ^ r) for i in range(count)]


def body(
    video_tokens,
    norm_gain,
    norm_bias,
    qkv_weight,
    frame_counts,
    clip_starts,
    frame_kept,
    attended_grad,
):
    tm_count, dp_count = lax.axis_size("tm"), lax.axis_size("dp")
    nz = dp_count // CORES
    _, frames, patches, width = video_tokens.shape
    joined = attended_grad.shape[3]
    shard, columns = qkv_weight.shape
    patches_dev = -(-patches // tm_count)
    group = max(2, 128 // (frames * tm_count))
    chunks = chunk_sizes(patches_dev, group, 2)
    dp = lax.axis_index("dp")

    def swap(array, r):
        return lax.ppermute(array, "tm", partner(tm_count, r))

    spare = ((0, tm_count * patches_dev - patches), (0, 0), (0, 0))
    tokens = jnp.pad(video_tokens[0].transpose(1, 0, 2), spare)
    upstream = jnp.pad(attended_grad[0].transpose(1, 0, 2), spare)
    offsets = [sum(chunks[:c]) for c in range(len(chunks))]
    lines = jnp.tile(jnp.stack([norm_gain, norm_bias]), (1, -(-columns // shard)))[:, :columns]

    def shift(array, k):
        hops = [(i, (i + CORES * k) % dp_count) for i in range(dp_count)]
        return lax.ppermute(array, "dp", hops)

    gathered = []
    for c, size in enumerate(chunks):
        more = (qkv_weight, lines) if c == 0 else ()
        blocks = pack(tm_count, patches_dev, offsets[c], size, tokens, upstream, *more)
        if c == 0:
            along = [blocks[0]] + [shift(blocks[0], k) for k in range(1, nz)]
            blocks = blocks[1:]
        blocks = [swap(part, r + 1) for r, part in enumerate(blocks)]
        if c == 0:
            along, blocks = lax.optimization_barrier((along, blocks))
            pieces = along + [lax.ppermute(jnp.stack(along), "dp", partner(dp_count, 1))]
        gathered.append(blocks)

    facts = (frame_counts, clip_starts, frame_kept)
    results, before = [], None
    for c, blocks in enumerate(gathered):
        first, last = c == 0, c == len(chunks) - 1
        got = chunk(
            tm_count,
            dp_count,
            group,
            patches_dev,
            offsets[c],
            first,
            last,
            facts,
            pieces,
            (tokens, upstream, blocks),
            before,
        )
        results.append([swap(part, r + 1) for r, part in enumerate(got[: tm_count - 1])])
        mixed, grads = got[tm_count - 1 : tm_count + 1]
        before = (got[tm_count + 1], got[tm_count + 2], mixed, grads)
    keep, send = got[-4:-2], got[-2:]

    send, results[0] = lax.optimization_barrier((send, results[0]))
    others = [lax.ppermute(part, "dp", partner(dp_count, 1)) for part in send]
    halves = []
    for mine, other in zip(keep, others):
        blocks = [
            lax.optimization_barrier((mine[k].astype(f32) + other[k].astype(f32)).astype(bf16))
            for k in range(nz)
        ]
        half = blocks[0].astype(f32)
        for k in range(1, nz):
            half = half + shift(blocks[k], k).astype(f32)
        halves.append(half)
    halves[0], results[-1] = lax.optimization_barrier((halves[0], results[-1]))
    summed = []
    for half in halves:
        r = 1
        while r < tm_count:
            mine = lax.optimization_barrier(half.astype(bf16))
            half = mine.astype(f32) + swap(mine, r).astype(f32)
            r *= 2
        summed.append(half)

    for c, blocks in enumerate(results):
        mixed, grads = unpack(
            tm_count, patches_dev, offsets[c], chunks[c], mixed, grads, blocks
        )
    attended = mixed[:patches].transpose(1, 0, 2)[None]
    tokens_grad = grads[:patches].transpose(1, 0, 2)[None]
    rest = shard - summed[0].shape[0]
    weight_total = jnp.concatenate([summed[0], summed[1][:rest]], axis=0)
    gain_total = lax.dynamic_slice(summed[1][rest], (dp * shard,), (shard,))
    bias_total = lax.dynamic_slice(summed[1][rest + 1], (dp * shard,), (shard,))
    return (attended, tokens_grad, weight_total, gain_total, bias_total)


def solution(mesh):
    placed = (
        P("dp", "tm", None, None),
        P("dp"),
        P("dp"),
        P("dp", None),
        P("dp"),
        P("dp", None),
        P("dp", None),
        P("dp", "tm", None, None),
    )
    return jax.shard_map(
        body,
        mesh=mesh,
        in_specs=placed,
        out_specs=(
            P("dp", "tm", None, None),
            P("dp", "tm", None, None),
            P("dp", None),
            P("dp"),
            P("dp"),
        ),
        check_vma=False,
    )
```

```python
import functools

import jax
import jax.numpy as jnp
from jax import lax
from jax.experimental import pallas as pl
from jax.experimental.pallas import tpu as pltpu
from jax.sharding import PartitionSpec as P

HEADS = 6
BLOCK = 16
CORES = 2
EXTRA = 8

masked_value = -1e30
epsilon = 1e-05
vmem_limit = 56 * 1024 * 1024
f32 = jnp.float32
bf16 = jnp.bfloat16


def halving_order(count):
    order, bit = [0], count // 2
    while bit:
        order = order + [bit + k for k in order]
        bit //= 2
    return order


def round_up(value, step):
    return -(-value // step) * step


def chunk_sizes(patches_dev, group):
    whole = patches_dev // group
    second = (whole // 2) * group
    return [patches_dev - second, second]


anywhere = pl.BlockSpec(memory_space=pl.ANY)


def run_all(pairs, sems):
    copies = [pltpu.make_async_copy(a, b, sems.at[i]) for i, (a, b) in enumerate(pairs)]
    for copy in copies:
        copy.start()
    return copies


def pack_kernel(tm_count, patches_dev, offset, size, x_ref, grad_ref, *rest):
    sems = rest[-1]
    outs = rest[-tm_count:-1]
    width = x_ref.shape[2]
    me = lax.axis_index("tm")
    pairs = []
    for r in range(1, tm_count):
        place = pl.ds((me ^ r) * patches_dev + offset, size)
        pairs.append((x_ref.at[place], outs[r - 1].at[:, :, pl.ds(0, width)]))
        pairs.append(
            (grad_ref.at[place], outs[r - 1].at[:, :, pl.ds(width, grad_ref.shape[2])])
        )
    if len(rest) > tm_count:
        weight_ref, gain_ref, bias_ref, own_ref = rest[:4]
        shard, columns = weight_ref.shape
        pairs.append((weight_ref, own_ref.at[pl.ds(0, shard)]))
    copies = run_all(pairs, sems)
    if len(rest) > tm_count:
        row = lax.broadcasted_iota(jnp.int32, (EXTRA, columns), 0)
        owner = lax.broadcasted_iota(jnp.int32, (EXTRA, columns), 1) // shard
        spread = lambda ref: jnp.concatenate(
            [ref[...].astype(f32).reshape(1, shard)] * (columns // shard), axis=1
        )
        lines = jnp.where(row == 0, spread(gain_ref), jnp.where(row == 1, spread(bias_ref), 0.0))
        own_ref[shard:, :] = jnp.where(owner == lax.axis_index("dp"), lines, 0.0).astype(bf16)
    for copy in copies:
        copy.wait()


def pack(tm_count, patches_dev, offset, size, tokens, grads, weight=None, gain=None, bias=None):
    _, frames, width = tokens.shape
    total = width + grads.shape[2]
    in_vmem = pl.BlockSpec(memory_space=pltpu.VMEM)
    args, specs = [tokens, grads], [anywhere] * 2
    outs = [jax.ShapeDtypeStruct((size, frames, total), bf16)] * (tm_count - 1)
    if weight is not None:
        args += [weight, gain, bias]
        specs += [anywhere, in_vmem, in_vmem]
        shard, columns = weight.shape
        outs = [jax.ShapeDtypeStruct((shard + EXTRA, columns), bf16)] + outs
    return pl.pallas_call(
        functools.partial(pack_kernel, tm_count, patches_dev, offset, size),
        out_shape=outs,
        in_specs=specs,
        out_specs=[in_vmem] * len(outs),
        scratch_shapes=[pltpu.SemaphoreType.DMA((2 * tm_count,))],
        compiler_params=pltpu.CompilerParams(vmem_limit_bytes=vmem_limit),
    )(*args)


def unpack_kernel(tm_count, patches_dev, offset, size, *refs):
    ins = refs[2 : tm_count + 1]
    mixed_ref, grad_ref, held, sems, out_sems = refs[tm_count + 1 :]
    joined, width = mixed_ref.shape[2], grad_ref.shape[2]
    me = lax.axis_index("tm")
    arriving = run_all([(ins[r - 1], held.at[r - 1]) for r in range(1, tm_count)], sems)
    leaving = []
    for r in range(1, tm_count):
        place = pl.ds((me ^ r) * patches_dev + offset, size)
        arriving[r - 1].wait()
        for at, ref in ((0, mixed_ref), (joined, grad_ref)):
            copy = pltpu.make_async_copy(
                held.at[r - 1, :, :, pl.ds(at, ref.shape[2])],
                ref.at[place],
                out_sems.at[len(leaving)],
            )
            copy.start()
            leaving.append(copy)
    for copy in leaving:
        copy.wait()


def unpack(tm_count, patches_dev, offset, size, mixed, grads, blocks):
    return pl.pallas_call(
        functools.partial(unpack_kernel, tm_count, patches_dev, offset, size),
        out_shape=[
            jax.ShapeDtypeStruct(mixed.shape, bf16),
            jax.ShapeDtypeStruct(grads.shape, bf16),
        ],
        in_specs=[anywhere] * (tm_count + 1),
        out_specs=[anywhere] * 2,
        input_output_aliases={0: 0, 1: 1},
        scratch_shapes=[
            pltpu.VMEM((tm_count - 1,) + blocks[0].shape, bf16),
            pltpu.SemaphoreType.DMA((tm_count,)),
            pltpu.SemaphoreType.DMA((2 * tm_count,)),
        ],
        compiler_params=pltpu.CompilerParams(vmem_limit_bytes=vmem_limit),
    )(mixed, grads, *blocks)


def frame_facts(frame, count_ref, starts_ref, kept_ref):
    clip = jnp.zeros_like(frame)
    for b in range(1, starts_ref.shape[1]):
        clip = clip + jnp.where(frame >= b * BLOCK, starts_ref[0, b], 0)
    kept = jnp.zeros_like(frame)
    for g in range(kept_ref.shape[1]):
        kept = jnp.where(frame == g, kept_ref[0, g], kept)
    usable = (frame < count_ref[0]) & (kept == 1)
    return clip, usable


def chunk_kernel(
    tm_count,
    dp_count,
    frames,
    group,
    groups,
    patches_dev,
    offset,
    first,
    last,
    count_ref,
    starts_ref,
    kept_ref,
    *rest,
):
    nz = dp_count // CORES
    rest = list(rest)
    take = lambda n: [rest.pop(0) for _ in range(n)]
    pieces = take(nz + 1)
    x_ref, grad_ref = take(2)
    sources = take(tm_count - 1)
    if not first:
        before, before_ends = take(2)
        take(2)
    outs = take(tm_count - 1)
    mixed_ref, tokens_ref = take(2)
    sums = take(4) if last else take(2)
    (xs, weight, extra, normed, standard, proj, pgrad, back, acc, ends, tails, allow, sems) = rest
    size = sources[0].shape[0]
    width = weight.shape[0]
    columns = weight.shape[1]
    joined = columns // 3
    tokens = groups * group * frames * tm_count
    span = group * frames
    shard = width // dp_count
    me = lax.axis_index("tm")
    dp = lax.axis_index("dp")
    z, core = dp // CORES, dp % CORES

    started = []

    def bring(src, dst):
        copy = pltpu.make_async_copy(src, dst, sems.at[len(started)])
        copy.start()
        started.append(copy)
        return copy

    mine = pl.ds(me * patches_dev + offset, size)
    kept = pl.ds(0, size)
    rows_in = [
        bring(x_ref.at[mine], xs.at[0, kept, :, pl.ds(0, width)]),
        bring(grad_ref.at[mine], xs.at[0, kept, :, pl.ds(width, joined)]),
    ]
    rows_in += [bring(sources[r - 1], xs.at[r, kept]) for r in range(1, tm_count)]
    weights_in, lines_in = [], []
    for side in range(CORES):
        for k in range(nz):
            owner = lax.rem(z + nz - k, nz) * CORES + (core ^ side)
            piece = pieces[k] if side == 0 else pieces[nz].at[k]
            place = pl.ds(pl.multiple_of(owner * shard, shard), shard)
            weights_in.append(bring(piece.at[pl.ds(0, shard)], weight.at[place]))
            lines_in.append(bring(piece.at[pl.ds(shard, EXTRA)], extra.at[side * nz + k]))
    if not first:
        acc_in = [bring(before, acc), bring(before_ends, tails)]
    if xs.shape[1] > size:
        for r in range(tm_count):
            xs[r, size:] = jnp.zeros((xs.shape[1] - size,) + xs.shape[2:], bf16)

    row = lax.broadcasted_iota(jnp.int32, (tm_count * frames, tokens // groups), 0)
    lane = lax.broadcasted_iota(jnp.int32, (tm_count * frames, tokens // groups), 1)
    key_frame = (me ^ (row // frames)) * frames + row % frames
    query_frame = (me ^ (lane // span)) * frames + lane % frames
    key_clip, key_usable = frame_facts(key_frame, count_ref, starts_ref, kept_ref)
    query_clip, _ = frame_facts(query_frame, count_ref, starts_ref, kept_ref)
    ok = (key_clip == query_clip) & (key_usable | (key_frame == query_frame))
    allow[...] = jnp.where(ok, 1.0, 0.0)
    token = lax.broadcasted_iota(jnp.int32, (tokens // groups, 128), 0)
    token_frame = (me ^ (token // span)) * frames + token % frames
    token_valid = token_frame < count_ref[0]

    for copy in lines_in:
        copy.wait()
    gain = functools.reduce(
        lambda a, b: a + b, [extra[i, 0:1, :width].astype(f32) for i in range(dp_count)]
    )
    bias = functools.reduce(
        lambda a, b: a + b, [extra[i, 1:2, :width].astype(f32) for i in range(dp_count)]
    )
    for copy in rows_in:
        copy.wait()

    unit = tokens // groups

    def token_rows(j, cut):
        rows = pl.ds(j * group, group)
        return jnp.concatenate(
            [xs[r, rows, :, cut].astype(f32).reshape(span, -1) for r in range(tm_count)], axis=0
        )

    def put_rows(j, cut, values):
        rows = pl.ds(j * group, group)
        for r in range(tm_count):
            block = values[r * span : (r + 1) * span].reshape(group, frames, -1)
            back[r, rows, :, cut] = block.astype(bf16)

    @pl.loop(0, groups)
    def _(j):
        x = token_rows(j, slice(0, width))
        centred = x - jnp.mean(x, axis=-1, keepdims=True)
        inverse = lax.rsqrt(jnp.mean(centred * centred, axis=-1, keepdims=True) + epsilon)
        std = centred * inverse
        at = pl.ds(pl.multiple_of(j * unit, unit), unit)
        standard[at, :] = std
        ends[at, :] = jnp.broadcast_to(inverse, (unit, 128))
        normed[at, :] = (std * gain + bias).astype(bf16)

    for copy in weights_in:
        copy.wait()
    for part in range(3):
        cut = slice(part * joined, (part + 1) * joined)
        proj[:, cut] = jnp.dot(
            normed[...], weight[:, cut], preferred_element_type=f32
        ).astype(bf16)

    pairs = joined // 128
    wide = joined // HEADS
    scale = wide ** (-0.5)
    low = lax.broadcasted_iota(jnp.int32, (unit, 128), 1) < wide
    patch_lane = (lax.broadcasted_iota(jnp.int32, (1, unit), 1) // frames) % group

    def stack(block):
        zero = jnp.zeros_like(block)
        return jnp.concatenate(
            [jnp.where(low, block, zero), jnp.where(low, zero, block)], axis=0
        )

    def compact(full):
        parts = full.reshape(2, tm_count, group, frames, unit)
        got = parts[:, :, 0]
        for p in range(1, group):
            got = jnp.where(patch_lane == p, parts[:, :, p], got)
        return got.reshape(2, tm_count * frames, unit)

    def expand(small):
        small = small.reshape(2, tm_count, 1, frames, unit)
        pieces = [jnp.where(patch_lane == p, small, 0.0) for p in range(group)]
        return jnp.concatenate(pieces, axis=2).reshape(2 * unit, unit).astype(bf16)

    nt = (((1,), (1,)), ((), ()))
    tn = (((0,), (0,)), ((), ()))

    @pl.loop(0, groups)
    def _(j):
        at = pl.ds(pl.multiple_of(j * unit, unit), unit)
        allowed = allow[...] > 0.5
        every = range(pairs)
        cols = [slice(pair * 128, (pair + 1) * 128) for pair in every]
        cut = lambda part: [
            proj[at, part * joined + pair * 128 : part * joined + (pair + 1) * 128]
            for pair in every
        ]
        q2, k2, v2 = cut(0), cut(1), cut(2)
        up = [
            token_rows(j, slice(width + pair * 128, width + (pair + 1) * 128)) for pair in every
        ]
        up = [jnp.where(token_valid, u, 0.0).astype(bf16) for u in up]
        kcat, vcat = [stack(k) for k in k2], [stack(v) for v in v2]
        scores = [
            compact(lax.dot_general(kcat[i], q2[i], nt, preferred_element_type=f32))
            for i in every
        ]
        wgrad = [
            compact(lax.dot_general(vcat[i], up[i], nt, preferred_element_type=f32))
            for i in every
        ]
        probs = []
        for i in every:
            masked = jnp.where(allowed, scores[i] * scale, masked_value)
            shifted = jnp.exp(masked - jnp.max(masked, axis=1, keepdims=True))
            probs.append(shifted * (1.0 / jnp.sum(shifted, axis=1, keepdims=True)))
        full = [expand(p) for p in probs]
        sgrad = []
        for i in every:
            inner = jnp.sum(wgrad[i] * probs[i], axis=1, keepdims=True)
            sgrad.append(expand(probs[i] * (wgrad[i] - inner) * scale))
        for i in every:
            mixed = lax.dot_general(full[i], vcat[i], tn, preferred_element_type=f32)
            put_rows(j, cols[i], jnp.where(token_valid, mixed, 0.0))
            across = jnp.concatenate([full[i][:unit], full[i][unit:]], axis=1)
            value_grad = jnp.dot(across, stack(up[i]), preferred_element_type=f32)
            query_grad = lax.dot_general(sgrad[i], kcat[i], tn, preferred_element_type=f32)
            sacross = jnp.concatenate([sgrad[i][:unit], sgrad[i][unit:]], axis=1)
            key_grad = jnp.dot(sacross, stack(q2[i]), preferred_element_type=f32)
            for part, value in enumerate((query_grad, key_grad, value_grad)):
                place = slice(part * joined + i * 128, part * joined + (i + 1) * 128)
                pgrad[at, place] = value.astype(bf16)

    if not first:
        for copy in acc_in:
            copy.wait()
    else:
        tails[...] = jnp.zeros_like(tails)
    for part in range(3):
        cut = slice(part * joined, (part + 1) * joined)
        share = lax.dot_general(normed[...], pgrad[:, cut], tn, preferred_element_type=f32)
        if first:
            acc[:, cut] = share
        else:
            acc[:, cut] += share

    gone = []
    if not last:
        gone.append(bring(acc, sums[0]))
    normed[...] = lax.dot_general(
        pgrad[...], weight[...], nt, preferred_element_type=f32
    ).astype(bf16)

    @pl.loop(0, groups)
    def _(j):
        at = pl.ds(pl.multiple_of(j * unit, unit), unit)
        ngrad = normed[at, :].astype(f32)
        std = standard[at, :]
        product = ngrad * std
        tails[0:8, :] += jnp.sum(product.reshape(unit // 8, 8, width), axis=0)
        tails[8:16, :] += jnp.sum(ngrad.reshape(unit // 8, 8, width), axis=0)
        scaled = ngrad * gain
        grad = ends[at, 0:1] * (
            scaled
            - jnp.mean(scaled, axis=-1, keepdims=True)
            - std * jnp.mean(product * gain, axis=-1, keepdims=True)
        )
        put_rows(j, slice(joined, columns), grad)

    gone += [bring(back.at[r, kept], outs[r - 1]) for r in range(1, tm_count)]
    gone.append(bring(back.at[0, kept, :, pl.ds(0, joined)], mixed_ref.at[mine]))
    gone.append(bring(back.at[0, kept, :, pl.ds(joined, width)], tokens_ref.at[mine]))
    if not last:
        gone.append(bring(tails, sums[1]))
    else:
        cut = sums[0].shape[1]
        extra_rows = jnp.concatenate(
            [
                jnp.sum(tails[0:8, :], axis=0, keepdims=True),
                jnp.sum(tails[8:16, :], axis=0, keepdims=True),
                jnp.zeros((EXTRA - 2, width), f32),
            ],
            axis=0,
        ).astype(bf16)
        for k, far in enumerate(halving_order(nz)):
            owner = (z ^ far) * CORES
            for refs, side in ((sums[:2], core), (sums[2:], 1 - core)):
                start = pl.multiple_of((owner + side) * shard, shard)
                refs[0][k] = acc[pl.ds(start, cut), :].astype(bf16)
                refs[1][k, : shard - cut, :] = acc[
                    pl.ds(pl.multiple_of(start + cut, 16), shard - cut), :
                ].astype(bf16)
                refs[1][k, shard - cut :, :width] = extra_rows
                refs[1][k, shard - cut :, width:] = jnp.zeros((EXTRA, columns - width), bf16)
    for copy in gone:
        copy.wait()


def chunk(
    tm_count, dp_count, group, patches_dev, offset, first, last, facts, pieces, sources, before
):
    tokens_in, grads_in, blocks = sources
    size, frames, total = blocks[0].shape
    shard, columns = pieces[0].shape[0] - EXTRA, pieces[0].shape[1]
    width = shard * dp_count
    groups = -(-size // group)
    tokens = groups * group * frames * tm_count
    nz = dp_count // CORES
    outs = [jax.ShapeDtypeStruct((size, frames, total), bf16)] * (tm_count - 1)
    outs += [
        jax.ShapeDtypeStruct(grads_in.shape, bf16),
        jax.ShapeDtypeStruct(tokens_in.shape, bf16),
    ]
    out_specs = [anywhere] * len(outs)
    if last:
        cut = round_up(shard // 2, 16)
        for _ in range(2):
            outs.append(jax.ShapeDtypeStruct((nz, cut, columns), bf16))
            outs.append(jax.ShapeDtypeStruct((nz, shard - cut + EXTRA, columns), bf16))
        out_specs += [pl.BlockSpec(memory_space=pltpu.VMEM)] * 4
    else:
        outs.append(jax.ShapeDtypeStruct((width, columns), f32))
        outs.append(jax.ShapeDtypeStruct((16, width), f32))
        out_specs += [anywhere] * 2
    args = list(facts) + list(pieces) + [tokens_in, grads_in] + list(blocks)
    aliases = {}
    if not first:
        args += list(before)
        aliases = {len(args) - 2: tm_count - 1, len(args) - 1: tm_count}
    rows = (tm_count, groups * group, frames, total)
    scratch = [
        pltpu.VMEM(rows, bf16),
        pltpu.VMEM((width, columns), bf16),
        pltpu.VMEM((dp_count, EXTRA, columns), bf16),
        pltpu.VMEM((tokens, width), bf16),
        pltpu.VMEM((tokens, width), f32),
        pltpu.VMEM((tokens, columns), bf16),
        pltpu.VMEM((tokens, columns), bf16),
        pltpu.VMEM(rows, bf16),
        pltpu.VMEM((width, columns), f32),
        pltpu.VMEM((tokens, 128), f32),
        pltpu.VMEM((16, width), f32),
        pltpu.VMEM((tm_count * frames, tokens // groups), f32),
        pltpu.SemaphoreType.DMA((2 * tm_count + 2 * dp_count + 12,)),
    ]
    return pl.pallas_call(
        functools.partial(
            chunk_kernel,
            tm_count,
            dp_count,
            frames,
            group,
            groups,
            patches_dev,
            offset,
            first,
            last,
        ),
        out_shape=outs,
        in_specs=[pl.BlockSpec(memory_space=pltpu.SMEM)] * 3 + [anywhere] * (len(args) - 3),
        out_specs=out_specs,
        scratch_shapes=scratch,
        input_output_aliases=aliases,
        compiler_params=pltpu.CompilerParams(vmem_limit_bytes=vmem_limit),
    )(*args)


def partner(count, r):
    return [(i, i ^ r) for i in range(count)]


def body(
    video_tokens,
    norm_gain,
    norm_bias,
    qkv_weight,
    frame_counts,
    clip_starts,
    frame_kept,
    attended_grad,
):
    tm_count, dp_count = lax.axis_size("tm"), lax.axis_size("dp")
    nz = dp_count // CORES
    _, frames, patches, width = video_tokens.shape
    joined = attended_grad.shape[3]
    shard, columns = qkv_weight.shape
    patches_dev = -(-patches // tm_count)
    group = max(2, 128 // (frames * tm_count))
    chunks = chunk_sizes(patches_dev, group)
    dp = lax.axis_index("dp")

    def swap(array, r):
        return lax.ppermute(array, "tm", partner(tm_count, r))

    spare = ((0, tm_count * patches_dev - patches), (0, 0), (0, 0))
    tokens = jnp.pad(video_tokens[0].transpose(1, 0, 2), spare)
    upstream = jnp.pad(attended_grad[0].transpose(1, 0, 2), spare)
    offsets = [sum(chunks[:c]) for c in range(len(chunks))]

    def shift(array, k):
        hops = [(i, (i + CORES * k) % dp_count) for i in range(dp_count)]
        return lax.ppermute(array, "dp", hops)

    blocks = [
        pack(tm_count, patches_dev, offset, size, tokens, upstream, *more)
        for offset, size, more in zip(offsets, chunks, ((qkv_weight, norm_gain, norm_bias), ()))
    ]
    own, early, late = blocks[0][0], list(blocks[0][1:]), blocks[1]
    along = [own] + [shift(own, k) for k in range(1, nz)]
    early[-1], along[1] = lax.optimization_barrier((early[-1], along[1]))
    early = [swap(part, r + 1) for r, part in enumerate(early)]
    along, early, late = lax.optimization_barrier((along, early, late))
    pieces = along + [lax.ppermute(jnp.stack(along), "dp", partner(dp_count, 1))]
    gathered = [early, [swap(part, r + 1) for r, part in enumerate(late)]]

    facts = (frame_counts, clip_starts, frame_kept)
    results, before = [], None
    for c in range(len(chunks)):
        blocks = gathered[c]
        first, last = c == 0, c == len(chunks) - 1
        got = chunk(
            tm_count,
            dp_count,
            group,
            patches_dev,
            offsets[c],
            first,
            last,
            facts,
            pieces,
            (tokens, upstream, blocks),
            before,
        )
        leaving = got[: tm_count - 1]
        if first:
            leaving, gathered[1] = lax.optimization_barrier((leaving, gathered[1]))
        results.append([swap(part, r + 1) for r, part in enumerate(leaving)])
        mixed, grads = got[tm_count - 1 : tm_count + 1]
        before = (got[tm_count + 1], got[tm_count + 2], mixed, grads)
    keep, send = got[-4:-2], got[-2:]

    send, results[0] = lax.optimization_barrier((send, results[0]))
    others = [lax.ppermute(part, "dp", partner(dp_count, 1)) for part in send]
    others, results[0] = lax.optimization_barrier((others, results[0]))
    halves = []
    for mine, other in zip(keep, others):
        left, bit = nz, 1
        half = mine.astype(f32) + other.astype(f32)
        while bit < nz:
            left //= 2
            gone = lax.optimization_barrier(half[left:].astype(bf16))
            got = lax.ppermute(gone, "dp", partner(dp_count, CORES * bit))
            half = half[:left] + got.astype(f32)
            bit *= 2
        halves.append(half[0])
    halves[0], results[-1] = lax.optimization_barrier((halves[0], results[-1]))
    summed = []
    for half in halves:
        r = 1
        while r < tm_count:
            mine = lax.optimization_barrier(half.astype(bf16))
            half = mine.astype(f32) + swap(mine, r).astype(f32)
            r *= 2
        summed.append(half)

    for c, blocks in enumerate(results):
        mixed, grads = unpack(
            tm_count, patches_dev, offsets[c], chunks[c], mixed, grads, blocks
        )
    attended = mixed[:patches].transpose(1, 0, 2)[None]
    tokens_grad = grads[:patches].transpose(1, 0, 2)[None]
    rest = shard - summed[0].shape[0]
    weight_total = jnp.concatenate([summed[0], summed[1][:rest]], axis=0)
    gain_total = lax.dynamic_slice(summed[1][rest], (dp * shard,), (shard,))
    bias_total = lax.dynamic_slice(summed[1][rest + 1], (dp * shard,), (shard,))
    return (attended, tokens_grad, weight_total, gain_total, bias_total)


def solution(mesh):
    placed = (
        P("dp", "tm", None, None),
        P("dp"),
        P("dp"),
        P("dp", None),
        P("dp"),
        P("dp", None),
        P("dp", None),
        P("dp", "tm", None, None),
    )
    return jax.shard_map(
        body,
        mesh=mesh,
        in_specs=placed,
        out_specs=(
            P("dp", "tm", None, None),
            P("dp", "tm", None, None),
            P("dp", None),
            P("dp"),
            P("dp"),
        ),
        check_vma=False,
    )
```

```python
import functools

import jax
import jax.numpy as jnp
from jax import lax
from jax.experimental import pallas as pl
from jax.experimental.pallas import tpu as pltpu
from jax.sharding import PartitionSpec as P

HEADS = 6
BLOCK = 16
CORES = 2
EXTRA = 8

masked_value = -1e30
epsilon = 1e-05
vmem_limit = 56 * 1024 * 1024
f32 = jnp.float32
bf16 = jnp.bfloat16


def halving_order(count):
    order, bit = [0], count // 2
    while bit:
        order = order + [bit + k for k in order]
        bit //= 2
    return order


def round_up(value, step):
    return -(-value // step) * step


def chunk_sizes(patches_dev, group):
    whole = patches_dev // group
    second = (whole // 2) * group
    return [patches_dev - second, second]


anywhere = pl.BlockSpec(memory_space=pl.ANY)


def run_all(pairs, sems):
    copies = [pltpu.make_async_copy(a, b, sems.at[i]) for i, (a, b) in enumerate(pairs)]
    for copy in copies:
        copy.start()
    return copies


def pack_kernel(tm_count, patches_dev, offset, size, x_ref, grad_ref, *rest):
    sems = rest[-1]
    outs = rest[-tm_count:-1]
    width = x_ref.shape[2]
    me = lax.axis_index("tm")
    pairs = []
    for r in range(1, tm_count):
        place = pl.ds((me ^ r) * patches_dev + offset, size)
        pairs.append((x_ref.at[place], outs[r - 1].at[:, :, pl.ds(0, width)]))
        pairs.append(
            (grad_ref.at[place], outs[r - 1].at[:, :, pl.ds(width, grad_ref.shape[2])])
        )
    if len(rest) > tm_count:
        weight_ref, gain_ref, bias_ref, own_ref = rest[:4]
        shard, columns = weight_ref.shape
        pairs.append((weight_ref, own_ref.at[pl.ds(0, shard)]))
    copies = run_all(pairs, sems)
    if len(rest) > tm_count:
        row = lax.broadcasted_iota(jnp.int32, (EXTRA, columns), 0)
        owner = lax.broadcasted_iota(jnp.int32, (EXTRA, columns), 1) // shard
        spread = lambda ref: jnp.concatenate(
            [ref[...].astype(f32).reshape(1, shard)] * (columns // shard), axis=1
        )
        lines = jnp.where(row == 0, spread(gain_ref), jnp.where(row == 1, spread(bias_ref), 0.0))
        own_ref[shard:, :] = jnp.where(owner == lax.axis_index("dp"), lines, 0.0).astype(bf16)
    for copy in copies:
        copy.wait()


def pack(tm_count, patches_dev, offset, size, tokens, grads, weight=None, gain=None, bias=None):
    _, frames, width = tokens.shape
    total = width + grads.shape[2]
    in_vmem = pl.BlockSpec(memory_space=pltpu.VMEM)
    args, specs = [tokens, grads], [anywhere] * 2
    outs = [jax.ShapeDtypeStruct((size, frames, total), bf16)] * (tm_count - 1)
    if weight is not None:
        args += [weight, gain, bias]
        specs += [anywhere, in_vmem, in_vmem]
        shard, columns = weight.shape
        outs = [jax.ShapeDtypeStruct((shard + EXTRA, columns), bf16)] + outs
    return pl.pallas_call(
        functools.partial(pack_kernel, tm_count, patches_dev, offset, size),
        out_shape=outs,
        in_specs=specs,
        out_specs=[in_vmem] * len(outs),
        scratch_shapes=[pltpu.SemaphoreType.DMA((2 * tm_count,))],
        compiler_params=pltpu.CompilerParams(vmem_limit_bytes=vmem_limit),
    )(*args)


def unpack_kernel(tm_count, patches_dev, offset, size, *refs):
    ins = refs[2 : tm_count + 1]
    mixed_ref, grad_ref, held, sems, out_sems = refs[tm_count + 1 :]
    joined, width = mixed_ref.shape[2], grad_ref.shape[2]
    me = lax.axis_index("tm")
    arriving = run_all([(ins[r - 1], held.at[r - 1]) for r in range(1, tm_count)], sems)
    leaving = []
    for r in range(1, tm_count):
        place = pl.ds((me ^ r) * patches_dev + offset, size)
        arriving[r - 1].wait()
        for at, ref in ((0, mixed_ref), (joined, grad_ref)):
            copy = pltpu.make_async_copy(
                held.at[r - 1, :, :, pl.ds(at, ref.shape[2])],
                ref.at[place],
                out_sems.at[len(leaving)],
            )
            copy.start()
            leaving.append(copy)
    for copy in leaving:
        copy.wait()


def unpack(tm_count, patches_dev, offset, size, mixed, grads, blocks):
    return pl.pallas_call(
        functools.partial(unpack_kernel, tm_count, patches_dev, offset, size),
        out_shape=[
            jax.ShapeDtypeStruct(mixed.shape, bf16),
            jax.ShapeDtypeStruct(grads.shape, bf16),
        ],
        in_specs=[anywhere] * (tm_count + 1),
        out_specs=[anywhere] * 2,
        input_output_aliases={0: 0, 1: 1},
        scratch_shapes=[
            pltpu.VMEM((tm_count - 1,) + blocks[0].shape, bf16),
            pltpu.SemaphoreType.DMA((tm_count,)),
            pltpu.SemaphoreType.DMA((2 * tm_count,)),
        ],
        compiler_params=pltpu.CompilerParams(vmem_limit_bytes=vmem_limit),
    )(mixed, grads, *blocks)


def frame_facts(frame, count_ref, starts_ref, kept_ref):
    clip = jnp.zeros_like(frame)
    for b in range(1, starts_ref.shape[1]):
        clip = clip + jnp.where(frame >= b * BLOCK, starts_ref[0, b], 0)
    kept = jnp.zeros_like(frame)
    for g in range(kept_ref.shape[1]):
        kept = jnp.where(frame == g, kept_ref[0, g], kept)
    usable = (frame < count_ref[0]) & (kept == 1)
    return clip, usable


def chunk_kernel(
    tm_count,
    dp_count,
    frames,
    group,
    groups,
    patches_dev,
    offset,
    first,
    last,
    count_ref,
    starts_ref,
    kept_ref,
    *rest,
):
    nz = dp_count // CORES
    rest = list(rest)
    take = lambda n: [rest.pop(0) for _ in range(n)]
    pieces = take(nz + 1)
    x_ref, grad_ref = take(2)
    sources = take(tm_count - 1)
    if not first:
        before, before_ends = take(2)
        take(2)
    outs = take(tm_count - 1)
    mixed_ref, tokens_ref = take(2)
    sums = take(4) if last else take(2)
    (xs, weight, extra, normed, standard, proj, pgrad, back, acc, ends, tails, allow, sems) = rest
    size = sources[0].shape[0]
    width = weight.shape[0]
    columns = weight.shape[1]
    joined = columns // 3
    tokens = groups * group * frames * tm_count
    span = group * frames
    shard = width // dp_count
    me = lax.axis_index("tm")
    dp = lax.axis_index("dp")
    z, core = dp // CORES, dp % CORES

    started = []

    def bring(src, dst):
        copy = pltpu.make_async_copy(src, dst, sems.at[len(started)])
        copy.start()
        started.append(copy)
        return copy

    mine = pl.ds(me * patches_dev + offset, size)
    kept = pl.ds(0, size)
    rows_in = [
        bring(x_ref.at[mine], xs.at[0, kept, :, pl.ds(0, width)]),
        bring(grad_ref.at[mine], xs.at[0, kept, :, pl.ds(width, joined)]),
    ]
    rows_in += [bring(sources[r - 1], xs.at[r, kept]) for r in range(1, tm_count)]
    weights_in, lines_in = [], []
    for side in range(CORES):
        for k in range(nz):
            owner = (z ^ k) * CORES + (core ^ side)
            piece = pieces[k] if side == 0 else pieces[nz].at[k]
            place = pl.ds(pl.multiple_of(owner * shard, shard), shard)
            weights_in.append(bring(piece.at[pl.ds(0, shard)], weight.at[place]))
            lines_in.append(bring(piece.at[pl.ds(shard, EXTRA)], extra.at[side * nz + k]))
    if not first:
        acc_in = [bring(before, acc), bring(before_ends, tails)]
    if xs.shape[1] > size:
        for r in range(tm_count):
            xs[r, size:] = jnp.zeros((xs.shape[1] - size,) + xs.shape[2:], bf16)

    row = lax.broadcasted_iota(jnp.int32, (tm_count * frames, tokens // groups), 0)
    lane = lax.broadcasted_iota(jnp.int32, (tm_count * frames, tokens // groups), 1)
    key_frame = (me ^ (row // frames)) * frames + row % frames
    query_frame = (me ^ (lane // span)) * frames + lane % frames
    key_clip, key_usable = frame_facts(key_frame, count_ref, starts_ref, kept_ref)
    query_clip, _ = frame_facts(query_frame, count_ref, starts_ref, kept_ref)
    ok = (key_clip == query_clip) & (key_usable | (key_frame == query_frame))
    allow[...] = jnp.where(ok, 1.0, 0.0)
    token = lax.broadcasted_iota(jnp.int32, (tokens // groups, 128), 0)
    token_frame = (me ^ (token // span)) * frames + token % frames
    token_valid = token_frame < count_ref[0]

    for copy in lines_in:
        copy.wait()
    gain = functools.reduce(
        lambda a, b: a + b, [extra[i, 0:1, :width].astype(f32) for i in range(dp_count)]
    )
    bias = functools.reduce(
        lambda a, b: a + b, [extra[i, 1:2, :width].astype(f32) for i in range(dp_count)]
    )
    for copy in rows_in:
        copy.wait()

    unit = tokens // groups

    def token_rows(j, cut):
        rows = pl.ds(j * group, group)
        return jnp.concatenate(
            [xs[r, rows, :, cut].astype(f32).reshape(span, -1) for r in range(tm_count)], axis=0
        )

    def put_rows(j, cut, values):
        rows = pl.ds(j * group, group)
        for r in range(tm_count):
            block = values[r * span : (r + 1) * span].reshape(group, frames, -1)
            back[r, rows, :, cut] = block.astype(bf16)

    @pl.loop(0, groups)
    def _(j):
        x = token_rows(j, slice(0, width))
        centred = x - jnp.mean(x, axis=-1, keepdims=True)
        inverse = lax.rsqrt(jnp.mean(centred * centred, axis=-1, keepdims=True) + epsilon)
        std = centred * inverse
        at = pl.ds(pl.multiple_of(j * unit, unit), unit)
        standard[at, :] = std
        ends[at, :] = jnp.broadcast_to(inverse, (unit, 128))
        normed[at, :] = (std * gain + bias).astype(bf16)

    for copy in weights_in:
        copy.wait()
    cuts = [slice(at, min(at + 512, columns)) for at in range(0, columns, 512)]
    for cut in cuts:
        proj[:, cut] = jnp.dot(
            normed[...], weight[:, cut], preferred_element_type=f32
        ).astype(bf16)

    pairs = joined // 128
    wide = joined // HEADS
    scale = wide ** (-0.5)
    low = lax.broadcasted_iota(jnp.int32, (unit, 128), 1) < wide
    patch_lane = (lax.broadcasted_iota(jnp.int32, (1, unit), 1) // frames) % group

    def stack(block):
        zero = jnp.zeros_like(block)
        return jnp.concatenate(
            [jnp.where(low, block, zero), jnp.where(low, zero, block)], axis=0
        )

    def compact(full):
        parts = full.reshape(2, tm_count, group, frames, unit)
        got = parts[:, :, 0]
        for p in range(1, group):
            got = jnp.where(patch_lane == p, parts[:, :, p], got)
        return got.reshape(2, tm_count * frames, unit)

    def expand(small):
        small = small.reshape(2, tm_count, 1, frames, unit)
        pieces = [jnp.where(patch_lane == p, small, 0.0) for p in range(group)]
        return jnp.concatenate(pieces, axis=2).reshape(2 * unit, unit).astype(bf16)

    nt = (((1,), (1,)), ((), ()))
    tn = (((0,), (0,)), ((), ()))

    @pl.loop(0, groups)
    def _(j):
        at = pl.ds(pl.multiple_of(j * unit, unit), unit)
        allowed = allow[...] > 0.5
        every = range(pairs)
        cols = [slice(pair * 128, (pair + 1) * 128) for pair in every]
        cut = lambda part: [
            proj[at, part * joined + pair * 128 : part * joined + (pair + 1) * 128]
            for pair in every
        ]
        q2, k2, v2 = cut(0), cut(1), cut(2)
        up = [
            token_rows(j, slice(width + pair * 128, width + (pair + 1) * 128)) for pair in every
        ]
        up = [jnp.where(token_valid, u, 0.0).astype(bf16) for u in up]
        kcat, vcat = [stack(k) for k in k2], [stack(v) for v in v2]
        scores = [
            compact(lax.dot_general(kcat[i], q2[i], nt, preferred_element_type=f32))
            for i in every
        ]
        wgrad = [
            compact(lax.dot_general(vcat[i], up[i], nt, preferred_element_type=f32))
            for i in every
        ]
        probs = []
        for i in every:
            masked = jnp.where(allowed, scores[i] * scale, masked_value)
            shifted = jnp.exp(masked - jnp.max(masked, axis=1, keepdims=True))
            probs.append(shifted * (1.0 / jnp.sum(shifted, axis=1, keepdims=True)))
        full = [expand(p) for p in probs]
        sgrad = []
        for i in every:
            inner = jnp.sum(wgrad[i] * probs[i], axis=1, keepdims=True)
            sgrad.append(expand(probs[i] * (wgrad[i] - inner) * scale))
        for i in every:
            mixed = lax.dot_general(full[i], vcat[i], tn, preferred_element_type=f32)
            put_rows(j, cols[i], jnp.where(token_valid, mixed, 0.0))
            across = jnp.concatenate([full[i][:unit], full[i][unit:]], axis=1)
            value_grad = jnp.dot(across, stack(up[i]), preferred_element_type=f32)
            query_grad = lax.dot_general(sgrad[i], kcat[i], tn, preferred_element_type=f32)
            sacross = jnp.concatenate([sgrad[i][:unit], sgrad[i][unit:]], axis=1)
            key_grad = jnp.dot(sacross, stack(q2[i]), preferred_element_type=f32)
            for part, value in enumerate((query_grad, key_grad, value_grad)):
                place = slice(part * joined + i * 128, part * joined + (i + 1) * 128)
                pgrad[at, place] = value.astype(bf16)

    if not first:
        for copy in acc_in:
            copy.wait()
    else:
        tails[...] = jnp.zeros_like(tails)
    for cut in cuts:
        share = lax.dot_general(normed[...], pgrad[:, cut], tn, preferred_element_type=f32)
        if first:
            acc[:, cut] = share
        else:
            acc[:, cut] += share

    gone = []
    if not last:
        gone.append(bring(acc, sums[0]))
    normed[...] = lax.dot_general(
        pgrad[...], weight[...], nt, preferred_element_type=f32
    ).astype(bf16)

    def finish(j):
        at = pl.ds(pl.multiple_of(j * unit, unit), unit)
        ngrad = normed[at, :].astype(f32)
        std = standard[at, :]
        product = ngrad * std
        tails[0:8, :] += jnp.sum(product.reshape(unit // 8, 8, width), axis=0)
        tails[8:16, :] += jnp.sum(ngrad.reshape(unit // 8, 8, width), axis=0)
        scaled = ngrad * gain
        grad = ends[at, 0:1] * (
            scaled
            - jnp.mean(scaled, axis=-1, keepdims=True)
            - std * jnp.mean(product * gain, axis=-1, keepdims=True)
        )
        put_rows(j, slice(joined, columns), grad)

    middle = (groups + 1) // 2
    for low_group, high_group in ((0, middle), (middle, groups)):
        pl.loop(low_group, high_group)(finish)
        start = low_group * group
        count = min(high_group * group, size) - start
        here, there = pl.ds(start, count), pl.ds(me * patches_dev + offset + start, count)
        for r in range(1, tm_count):
            gone.append(bring(back.at[r, here], outs[r - 1].at[here]))
        gone.append(bring(back.at[0, here, :, pl.ds(0, joined)], mixed_ref.at[there]))
        gone.append(bring(back.at[0, here, :, pl.ds(joined, width)], tokens_ref.at[there]))
    if not last:
        gone.append(bring(tails, sums[1]))
    else:
        cut = sums[0].shape[1]
        extra_rows = jnp.concatenate(
            [
                jnp.sum(tails[0:8, :], axis=0, keepdims=True),
                jnp.sum(tails[8:16, :], axis=0, keepdims=True),
                jnp.zeros((EXTRA - 2, width), f32),
            ],
            axis=0,
        ).astype(bf16)
        for k, far in enumerate(halving_order(nz)):
            owner = (z ^ far) * CORES
            for refs, side in ((sums[:2], core), (sums[2:], 1 - core)):
                start = pl.multiple_of((owner + side) * shard, shard)
                refs[0][k] = acc[pl.ds(start, cut), :].astype(bf16)
                refs[1][k, : shard - cut, :] = acc[
                    pl.ds(pl.multiple_of(start + cut, 16), shard - cut), :
                ].astype(bf16)
                refs[1][k, shard - cut :, :width] = extra_rows
                refs[1][k, shard - cut :, width:] = jnp.zeros((EXTRA, columns - width), bf16)
    for copy in gone:
        copy.wait()


def chunk(
    tm_count, dp_count, group, patches_dev, offset, first, last, facts, pieces, sources, before
):
    tokens_in, grads_in, blocks = sources
    size, frames, total = blocks[0].shape
    shard, columns = pieces[0].shape[0] - EXTRA, pieces[0].shape[1]
    width = shard * dp_count
    groups = -(-size // group)
    tokens = groups * group * frames * tm_count
    nz = dp_count // CORES
    outs = [jax.ShapeDtypeStruct((size, frames, total), bf16)] * (tm_count - 1)
    outs += [
        jax.ShapeDtypeStruct(grads_in.shape, bf16),
        jax.ShapeDtypeStruct(tokens_in.shape, bf16),
    ]
    out_specs = [anywhere] * len(outs)
    if last:
        cut = round_up(shard // 2, 16)
        for _ in range(2):
            outs.append(jax.ShapeDtypeStruct((nz, cut, columns), bf16))
            outs.append(jax.ShapeDtypeStruct((nz, shard - cut + EXTRA, columns), bf16))
        out_specs += [pl.BlockSpec(memory_space=pltpu.VMEM)] * 4
    else:
        outs.append(jax.ShapeDtypeStruct((width, columns), f32))
        outs.append(jax.ShapeDtypeStruct((16, width), f32))
        out_specs += [anywhere] * 2
    args = list(facts) + list(pieces) + [tokens_in, grads_in] + list(blocks)
    aliases = {}
    if not first:
        args += list(before)
        aliases = {len(args) - 2: tm_count - 1, len(args) - 1: tm_count}
    rows = (tm_count, groups * group, frames, total)
    scratch = [
        pltpu.VMEM(rows, bf16),
        pltpu.VMEM((width, columns), bf16),
        pltpu.VMEM((dp_count, EXTRA, columns), bf16),
        pltpu.VMEM((tokens, width), bf16),
        pltpu.VMEM((tokens, width), f32),
        pltpu.VMEM((tokens, columns), bf16),
        pltpu.VMEM((tokens, columns), bf16),
        pltpu.VMEM(rows, bf16),
        pltpu.VMEM((width, columns), f32),
        pltpu.VMEM((tokens, 128), f32),
        pltpu.VMEM((16, width), f32),
        pltpu.VMEM((tm_count * frames, tokens // groups), f32),
        pltpu.SemaphoreType.DMA((3 * tm_count + 2 * dp_count + 14,)),
    ]
    return pl.pallas_call(
        functools.partial(
            chunk_kernel,
            tm_count,
            dp_count,
            frames,
            group,
            groups,
            patches_dev,
            offset,
            first,
            last,
        ),
        out_shape=outs,
        in_specs=[pl.BlockSpec(memory_space=pltpu.SMEM)] * 3 + [anywhere] * (len(args) - 3),
        out_specs=out_specs,
        scratch_shapes=scratch,
        input_output_aliases=aliases,
        compiler_params=pltpu.CompilerParams(vmem_limit_bytes=vmem_limit),
    )(*args)


def partner(count, r):
    return [(i, i ^ r) for i in range(count)]


def body(
    video_tokens,
    norm_gain,
    norm_bias,
    qkv_weight,
    frame_counts,
    clip_starts,
    frame_kept,
    attended_grad,
):
    tm_count, dp_count = lax.axis_size("tm"), lax.axis_size("dp")
    nz = dp_count // CORES
    _, frames, patches, width = video_tokens.shape
    joined = attended_grad.shape[3]
    shard, columns = qkv_weight.shape
    patches_dev = -(-patches // tm_count)
    group = max(2, 128 // (frames * tm_count))
    chunks = chunk_sizes(patches_dev, group)
    dp = lax.axis_index("dp")

    def swap(array, r):
        return lax.ppermute(array, "tm", partner(tm_count, r))

    spare = ((0, tm_count * patches_dev - patches), (0, 0), (0, 0))
    tokens = jnp.pad(video_tokens[0].transpose(1, 0, 2), spare)
    upstream = jnp.pad(attended_grad[0].transpose(1, 0, 2), spare)
    offsets = [sum(chunks[:c]) for c in range(len(chunks))]

    def across(array, k):
        return lax.ppermute(array, "dp", partner(dp_count, k))

    blocks = [
        pack(tm_count, patches_dev, offset, size, tokens, upstream, *more)
        for offset, size, more in zip(offsets, chunks, ((qkv_weight, norm_gain, norm_bias), ()))
    ]
    own, early, late = blocks[0][0], list(blocks[0][1:]), blocks[1]
    along, bit = {0: own}, nz // 2
    while bit:
        along.update({k + bit: across(along[k], CORES * bit) for k in sorted(along)})
        bit //= 2
    along = [along[k] for k in range(nz)]
    early = [swap(part, r + 1) for r, part in enumerate(early)]
    along, early, late = lax.optimization_barrier((along, early, late))
    pieces = along + [across(jnp.stack(along), 1)]
    gathered = [early, [swap(part, r + 1) for r, part in enumerate(late)]]

    facts = (frame_counts, clip_starts, frame_kept)
    results, before = [], None
    for c in range(len(chunks)):
        blocks = gathered[c]
        first, last = c == 0, c == len(chunks) - 1
        got = chunk(
            tm_count,
            dp_count,
            group,
            patches_dev,
            offsets[c],
            first,
            last,
            facts,
            pieces,
            (tokens, upstream, blocks),
            before,
        )
        leaving = got[: tm_count - 1]
        if first:
            leaving, gathered[1] = lax.optimization_barrier((leaving, gathered[1]))
        results.append([swap(part, r + 1) for r, part in enumerate(leaving)])
        mixed, grads = got[tm_count - 1 : tm_count + 1]
        before = (got[tm_count + 1], got[tm_count + 2], mixed, grads)
    keep, send = got[-4:-2], got[-2:]

    send, results[0] = lax.optimization_barrier((send, results[0]))
    others = [across(part, 1) for part in send]
    others, results[0] = lax.optimization_barrier((others, results[0]))
    halves = []
    for mine, other in zip(keep, others):
        left, bit = nz, 1
        half = mine.astype(f32) + other.astype(f32)
        while bit < nz:
            left //= 2
            gone = lax.optimization_barrier(half[left:].astype(bf16))
            got = across(gone, CORES * bit)
            half = half[:left] + got.astype(f32)
            bit *= 2
        halves.append(half[0])
    halves[0], results[-1] = lax.optimization_barrier((halves[0], results[-1]))
    summed = []
    for side, half in enumerate(halves):
        r = 1
        while r < tm_count:
            mine = lax.optimization_barrier(half.astype(bf16))
            got = swap(mine, r)
            if side == 0 and r == 1:
                got, results[-1] = lax.optimization_barrier((got, results[-1]))
            half = mine.astype(f32) + got.astype(f32)
            if side == 1 and 2 * r < tm_count:
                half += swap(mine, 2 * r).astype(f32) + swap(mine, 3 * r).astype(f32)
                r *= 2
            r *= 2
        summed.append(half)

    for c, blocks in enumerate(results):
        mixed, grads = unpack(
            tm_count, patches_dev, offsets[c], chunks[c], mixed, grads, blocks
        )
    attended = mixed[:patches].transpose(1, 0, 2)[None]
    tokens_grad = grads[:patches].transpose(1, 0, 2)[None]
    rest = shard - summed[0].shape[0]
    weight_total = jnp.concatenate([summed[0], summed[1][:rest]], axis=0)
    gain_total = lax.dynamic_slice(summed[1][rest], (dp * shard,), (shard,))
    bias_total = lax.dynamic_slice(summed[1][rest + 1], (dp * shard,), (shard,))
    return (attended, tokens_grad, weight_total, gain_total, bias_total)


def solution(mesh):
    placed = (
        P("dp", "tm", None, None),
        P("dp"),
        P("dp"),
        P("dp", None),
        P("dp"),
        P("dp", None),
        P("dp", None),
        P("dp", "tm", None, None),
    )
    return jax.shard_map(
        body,
        mesh=mesh,
        in_specs=placed,
        out_specs=(
            P("dp", "tm", None, None),
            P("dp", "tm", None, None),
            P("dp", None),
            P("dp"),
            P("dp"),
        ),
        check_vma=False,
    )
```

```python
import functools

import jax
import jax.numpy as jnp
from jax import lax
from jax.experimental import pallas as pl
from jax.experimental.pallas import tpu as pltpu
from jax.sharding import PartitionSpec as P

HEADS = 6
BLOCK = 16
CORES = 2
EXTRA = 8
CARRIED = 16

masked_value = -1e30
epsilon = 1e-05
vmem_limit = 56 * 1024 * 1024
f32 = jnp.float32
bf16 = jnp.bfloat16


def halving_order(count):
    order, bit = [0], count // 2
    while bit:
        order = order + [bit + k for k in order]
        bit //= 2
    return order


def round_up(value, step):
    return -(-value // step) * step


def chunk_sizes(patches_dev, group):
    whole = patches_dev // group
    second = (whole // 2) * group
    return [patches_dev - second, second]


anywhere = pl.BlockSpec(memory_space=pl.ANY)


def run_all(pairs, sems):
    copies = [pltpu.make_async_copy(a, b, sems.at[i]) for i, (a, b) in enumerate(pairs)]
    for copy in copies:
        copy.start()
    return copies


def pack_kernel(tm_count, patches_dev, offset, size, x_ref, grad_ref, *rest):
    sems = rest[-1]
    outs = rest[-tm_count:-1]
    width = x_ref.shape[2]
    me = lax.axis_index("tm")
    pairs = []
    for r in range(1, tm_count):
        place = pl.ds((me ^ r) * patches_dev + offset, size)
        pairs.append((x_ref.at[place], outs[r - 1].at[:, :, pl.ds(0, width)]))
        pairs.append(
            (grad_ref.at[place], outs[r - 1].at[:, :, pl.ds(width, grad_ref.shape[2])])
        )
    if len(rest) > tm_count:
        weight_ref, gain_ref, bias_ref, own_ref = rest[:4]
        shard, columns = weight_ref.shape
        pairs.append((weight_ref, own_ref.at[pl.ds(0, shard)]))
    copies = run_all(pairs, sems)
    if len(rest) > tm_count:
        row = lax.broadcasted_iota(jnp.int32, (EXTRA, columns), 0)
        owner = lax.broadcasted_iota(jnp.int32, (EXTRA, columns), 1) // shard
        spread = lambda ref: jnp.concatenate(
            [ref[...].astype(f32).reshape(1, shard)] * (columns // shard), axis=1
        )
        lines = jnp.where(row == 0, spread(gain_ref), jnp.where(row == 1, spread(bias_ref), 0.0))
        own_ref[shard:, :] = jnp.where(owner == lax.axis_index("dp"), lines, 0.0).astype(bf16)
    for copy in copies:
        copy.wait()


def pack(tm_count, patches_dev, offset, size, tokens, grads, weight=None, gain=None, bias=None):
    _, frames, width = tokens.shape
    total = width + grads.shape[2]
    in_vmem = pl.BlockSpec(memory_space=pltpu.VMEM)
    args, specs = [tokens, grads], [anywhere] * 2
    outs = [jax.ShapeDtypeStruct((size, frames, total), bf16)] * (tm_count - 1)
    if weight is not None:
        args += [weight, gain, bias]
        specs += [anywhere, in_vmem, in_vmem]
        shard, columns = weight.shape
        outs = [jax.ShapeDtypeStruct((shard + EXTRA, columns), bf16)] + outs
    return pl.pallas_call(
        functools.partial(pack_kernel, tm_count, patches_dev, offset, size),
        out_shape=outs,
        in_specs=specs,
        out_specs=[in_vmem] * len(outs),
        scratch_shapes=[pltpu.SemaphoreType.DMA((2 * tm_count,))],
        compiler_params=pltpu.CompilerParams(vmem_limit_bytes=vmem_limit),
    )(*args)


def unpack_kernel(tm_count, patches_dev, offset, size, *refs):
    ins = refs[2 : tm_count + 1]
    mixed_ref, grad_ref, held, sems, out_sems = refs[tm_count + 1 :]
    joined, width = mixed_ref.shape[2], grad_ref.shape[2]
    me = lax.axis_index("tm")
    arriving = run_all([(ins[r - 1], held.at[r - 1]) for r in range(1, tm_count)], sems)
    leaving = []
    for r in range(1, tm_count):
        place = pl.ds((me ^ r) * patches_dev + offset, size)
        arriving[r - 1].wait()
        for at, ref in ((0, mixed_ref), (joined, grad_ref)):
            copy = pltpu.make_async_copy(
                held.at[r - 1, :, :, pl.ds(at, ref.shape[2])],
                ref.at[place],
                out_sems.at[len(leaving)],
            )
            copy.start()
            leaving.append(copy)
    for copy in leaving:
        copy.wait()


def unpack(tm_count, patches_dev, offset, size, mixed, grads, blocks):
    return pl.pallas_call(
        functools.partial(unpack_kernel, tm_count, patches_dev, offset, size),
        out_shape=[
            jax.ShapeDtypeStruct(mixed.shape, bf16),
            jax.ShapeDtypeStruct(grads.shape, bf16),
        ],
        in_specs=[anywhere] * (tm_count + 1),
        out_specs=[anywhere] * 2,
        input_output_aliases={0: 0, 1: 1},
        scratch_shapes=[
            pltpu.VMEM((tm_count - 1,) + blocks[0].shape, bf16),
            pltpu.SemaphoreType.DMA((tm_count,)),
            pltpu.SemaphoreType.DMA((2 * tm_count,)),
        ],
        compiler_params=pltpu.CompilerParams(vmem_limit_bytes=vmem_limit),
    )(mixed, grads, *blocks)


def frame_facts(frame, count_ref, starts_ref, kept_ref):
    clip = jnp.zeros_like(frame)
    for b in range(1, starts_ref.shape[1]):
        clip = clip + jnp.where(frame >= b * BLOCK, starts_ref[0, b], 0)
    kept = jnp.zeros_like(frame)
    for g in range(kept_ref.shape[1]):
        kept = jnp.where(frame == g, kept_ref[0, g], kept)
    usable = (frame < count_ref[0]) & (kept == 1)
    return clip, usable


def chunk_kernel(
    tm_count,
    dp_count,
    frames,
    group,
    groups,
    patches_dev,
    offset,
    carry,
    first,
    last,
    count_ref,
    starts_ref,
    kept_ref,
    *rest,
):
    nz = dp_count // CORES
    rest = list(rest)
    take = lambda n: [rest.pop(0) for _ in range(n)]
    pieces = take(nz + 1)
    x_ref, grad_ref = take(2)
    sources = take(tm_count - 1)
    if not first:
        carried = take(tm_count - 1) if carry else []
        before, before_ends = take(2)
        take(2)
    outs = take(tm_count - 1)
    rests = take(tm_count - 1) if first and carry else []
    mixed_ref, tokens_ref = take(2)
    sums = take(4) if last else take(2)
    (xs, weight, extra, normed, standard, proj, pgrad, back, acc, ends, tails, allow, sems) = rest
    size = sources[0].shape[0]
    width = weight.shape[0]
    columns = weight.shape[1]
    joined = columns // 3
    tokens = groups * group * frames * tm_count
    span = group * frames
    shard = width // dp_count
    me = lax.axis_index("tm")
    dp = lax.axis_index("dp")
    z, core = dp // CORES, dp % CORES

    started = []

    def bring(src, dst):
        copy = pltpu.make_async_copy(src, dst, sems.at[len(started)])
        copy.start()
        started.append(copy)
        return copy

    mine = pl.ds(me * patches_dev + offset, size)
    kept = pl.ds(0, size)
    rows_in = [
        bring(x_ref.at[mine], xs.at[0, kept, :, pl.ds(0, width)]),
        bring(grad_ref.at[mine], xs.at[0, kept, :, pl.ds(width, joined)]),
    ]
    rows_in += [bring(sources[r - 1], xs.at[r, kept]) for r in range(1, tm_count)]
    weights_in, lines_in = [], []
    for side in range(CORES):
        for k in range(nz):
            owner = (z ^ k) * CORES + (core ^ side)
            piece = pieces[k] if side == 0 else pieces[nz].at[k]
            place = pl.ds(pl.multiple_of(owner * shard, shard), shard)
            weights_in.append(bring(piece.at[pl.ds(0, shard)], weight.at[place]))
            lines_in.append(bring(piece.at[pl.ds(shard, EXTRA)], extra.at[side * nz + k]))
    if not first:
        acc_in = [bring(before, acc), bring(before_ends, tails)]
    if xs.shape[1] > size:
        for r in range(tm_count):
            xs[r, size:] = jnp.zeros((xs.shape[1] - size,) + xs.shape[2:], bf16)

    row = lax.broadcasted_iota(jnp.int32, (tm_count * frames, tokens // groups), 0)
    lane = lax.broadcasted_iota(jnp.int32, (tm_count * frames, tokens // groups), 1)
    key_frame = (me ^ (row // frames)) * frames + row % frames
    query_frame = (me ^ (lane // span)) * frames + lane % frames
    key_clip, key_usable = frame_facts(key_frame, count_ref, starts_ref, kept_ref)
    query_clip, _ = frame_facts(query_frame, count_ref, starts_ref, kept_ref)
    ok = (key_clip == query_clip) & (key_usable | (key_frame == query_frame))
    allow[...] = jnp.where(ok, 1.0, 0.0)
    token = lax.broadcasted_iota(jnp.int32, (tokens // groups, 128), 0)
    token_frame = (me ^ (token // span)) * frames + token % frames
    token_valid = token_frame < count_ref[0]

    for copy in lines_in:
        copy.wait()
    gain = functools.reduce(
        lambda a, b: a + b, [extra[i, 0:1, :width].astype(f32) for i in range(dp_count)]
    )
    bias = functools.reduce(
        lambda a, b: a + b, [extra[i, 1:2, :width].astype(f32) for i in range(dp_count)]
    )
    for copy in rows_in:
        copy.wait()
    gone = []
    if not first:
        gone += [bring(ref, outs[r].at[pl.ds(0, carry)]) for r, ref in enumerate(carried)]

    unit = tokens // groups

    def token_rows(j, cut):
        rows = pl.ds(j * group, group)
        return jnp.concatenate(
            [xs[r, rows, :, cut].astype(f32).reshape(span, -1) for r in range(tm_count)], axis=0
        )

    def put_rows(j, cut, values):
        rows = pl.ds(j * group, group)
        for r in range(tm_count):
            block = values[r * span : (r + 1) * span].reshape(group, frames, -1)
            back[r, rows, :, cut] = block.astype(bf16)

    @pl.loop(0, groups, unroll=2)
    def _(j):
        x = token_rows(j, slice(0, width))
        centred = x - jnp.mean(x, axis=-1, keepdims=True)
        inverse = lax.rsqrt(jnp.mean(centred * centred, axis=-1, keepdims=True) + epsilon)
        std = centred * inverse
        at = pl.ds(pl.multiple_of(j * unit, unit), unit)
        standard[at, :] = std
        ends[at, :] = jnp.broadcast_to(inverse, (unit, 128))
        normed[at, :] = (std * gain + bias).astype(bf16)

    for copy in weights_in:
        copy.wait()
    cuts = [slice(at, min(at + 512, columns)) for at in range(0, columns, 512)]
    for cut in cuts:
        proj[:, cut] = jnp.dot(
            normed[...], weight[:, cut], preferred_element_type=f32
        ).astype(bf16)

    pairs = joined // 128
    wide = joined // HEADS
    scale = wide ** (-0.5)
    low = lax.broadcasted_iota(jnp.int32, (unit, 128), 1) < wide
    patch_lane = (lax.broadcasted_iota(jnp.int32, (1, unit), 1) // frames) % group

    def stack(block):
        zero = jnp.zeros_like(block)
        return jnp.concatenate(
            [jnp.where(low, block, zero), jnp.where(low, zero, block)], axis=0
        )

    def compact(full):
        parts = full.reshape(2, tm_count, group, frames, unit)
        got = parts[:, :, 0]
        for p in range(1, group):
            got = jnp.where(patch_lane == p, parts[:, :, p], got)
        return got.reshape(2, tm_count * frames, unit)

    def expand(small):
        small = small.reshape(2, tm_count, 1, frames, unit)
        pieces = [jnp.where(patch_lane == p, small, 0.0) for p in range(group)]
        return jnp.concatenate(pieces, axis=2).reshape(2 * unit, unit).astype(bf16)

    nt = (((1,), (1,)), ((), ()))
    tn = (((0,), (0,)), ((), ()))

    @pl.loop(0, groups, unroll=2)
    def _(j):
        at = pl.ds(pl.multiple_of(j * unit, unit), unit)
        allowed = allow[...] > 0.5
        every = range(pairs)
        cols = [slice(pair * 128, (pair + 1) * 128) for pair in every]
        cut = lambda part: [
            proj[at, part * joined + pair * 128 : part * joined + (pair + 1) * 128]
            for pair in every
        ]
        q2, k2, v2 = cut(0), cut(1), cut(2)
        up = [
            token_rows(j, slice(width + pair * 128, width + (pair + 1) * 128)) for pair in every
        ]
        up = [jnp.where(token_valid, u, 0.0).astype(bf16) for u in up]
        kcat, vcat = [stack(k) for k in k2], [stack(v) for v in v2]
        scores = [
            compact(lax.dot_general(kcat[i], q2[i], nt, preferred_element_type=f32))
            for i in every
        ]
        wgrad = [
            compact(lax.dot_general(vcat[i], up[i], nt, preferred_element_type=f32))
            for i in every
        ]
        probs = []
        for i in every:
            masked = jnp.where(allowed, scores[i] * scale, masked_value)
            shifted = jnp.exp(masked - jnp.max(masked, axis=1, keepdims=True))
            probs.append(shifted * (1.0 / jnp.sum(shifted, axis=1, keepdims=True)))
        full = [expand(p) for p in probs]
        sgrad = []
        for i in every:
            inner = jnp.sum(wgrad[i] * probs[i], axis=1, keepdims=True)
            sgrad.append(expand(probs[i] * (wgrad[i] - inner) * scale))
        for i in every:
            mixed = lax.dot_general(full[i], vcat[i], tn, preferred_element_type=f32)
            put_rows(j, cols[i], jnp.where(token_valid, mixed, 0.0))
            across = jnp.concatenate([full[i][:unit], full[i][unit:]], axis=1)
            value_grad = jnp.dot(across, stack(up[i]), preferred_element_type=f32)
            query_grad = lax.dot_general(sgrad[i], kcat[i], tn, preferred_element_type=f32)
            sacross = jnp.concatenate([sgrad[i][:unit], sgrad[i][unit:]], axis=1)
            key_grad = jnp.dot(sacross, stack(q2[i]), preferred_element_type=f32)
            for part, value in enumerate((query_grad, key_grad, value_grad)):
                place = slice(part * joined + i * 128, part * joined + (i + 1) * 128)
                pgrad[at, place] = value.astype(bf16)

    if not first:
        for copy in acc_in:
            copy.wait()
    else:
        tails[...] = jnp.zeros_like(tails)
    for cut in cuts:
        share = lax.dot_general(normed[...], pgrad[:, cut], tn, preferred_element_type=f32)
        if first:
            acc[:, cut] = share
        else:
            acc[:, cut] += share

    if not last:
        gone.append(bring(acc, sums[0]))
    else:
        cut = sums[0].shape[1]
        for k, far in enumerate(halving_order(nz)):
            owner = (z ^ far) * CORES
            for refs, side in ((sums[:2], core), (sums[2:], 1 - core)):
                start = pl.multiple_of((owner + side) * shard, shard)
                refs[0][k] = acc[pl.ds(start, cut), :].astype(bf16)
                refs[1][k, : shard - cut, :] = acc[
                    pl.ds(pl.multiple_of(start + cut, 16), shard - cut), :
                ].astype(bf16)
    normed[...] = lax.dot_general(
        pgrad[...], weight[...], nt, preferred_element_type=f32
    ).astype(bf16)

    def finish(j):
        at = pl.ds(pl.multiple_of(j * unit, unit), unit)
        ngrad = normed[at, :].astype(f32)
        std = standard[at, :]
        product = ngrad * std
        tails[0:8, :] += jnp.sum(product.reshape(unit // 8, 8, width), axis=0)
        tails[8:16, :] += jnp.sum(ngrad.reshape(unit // 8, 8, width), axis=0)
        scaled = ngrad * gain
        grad = ends[at, 0:1] * (
            scaled
            - jnp.mean(scaled, axis=-1, keepdims=True)
            - std * jnp.mean(product * gain, axis=-1, keepdims=True)
        )
        put_rows(j, slice(joined, columns), grad)

    middle = (groups + 1) // 2
    for low_group, high_group in ((0, middle), (middle, groups)):
        pl.loop(low_group, high_group, unroll=2)(finish)
        start = low_group * group
        count = min(high_group * group, size) - start
        here, there = pl.ds(start, count), pl.ds(me * patches_dev + offset + start, count)
        now = max(0, min(start + count, size - carry) - start) if first else count
        shift = 0 if first else carry
        for r in range(1, tm_count):
            if now:
                part = back.at[r, pl.ds(start, now)]
                gone.append(bring(part, outs[r - 1].at[pl.ds(start + shift, now)]))
            if now < count:
                part = back.at[r, pl.ds(start + now, count - now)]
                there_rest = pl.ds(start + now - (size - carry), count - now)
                gone.append(bring(part, rests[r - 1].at[there_rest]))
        gone.append(bring(back.at[0, here, :, pl.ds(0, joined)], mixed_ref.at[there]))
        gone.append(bring(back.at[0, here, :, pl.ds(joined, width)], tokens_ref.at[there]))
    if not last:
        gone.append(bring(tails, sums[1]))
    else:
        cut = sums[0].shape[1]
        extra_rows = jnp.concatenate(
            [
                jnp.sum(tails[0:8, :], axis=0, keepdims=True),
                jnp.sum(tails[8:16, :], axis=0, keepdims=True),
                jnp.zeros((EXTRA - 2, width), f32),
            ],
            axis=0,
        ).astype(bf16)
        for k in range(nz):
            for ref in (sums[1], sums[3]):
                ref[k, shard - cut :, :width] = extra_rows
                ref[k, shard - cut :, width:] = jnp.zeros((EXTRA, columns - width), bf16)
    for copy in gone:
        copy.wait()


def chunk(
    tm_count,
    dp_count,
    group,
    patches_dev,
    offset,
    carry,
    first,
    last,
    facts,
    pieces,
    sources,
    before,
):
    tokens_in, grads_in, blocks = sources
    size, frames, total = blocks[0].shape
    shard, columns = pieces[0].shape[0] - EXTRA, pieces[0].shape[1]
    width = shard * dp_count
    groups = -(-size // group)
    tokens = groups * group * frames * tm_count
    nz = dp_count // CORES
    leaving = size - carry if first else size + carry
    outs = [jax.ShapeDtypeStruct((leaving, frames, total), bf16)] * (tm_count - 1)
    if first and carry:
        outs += [jax.ShapeDtypeStruct((carry, frames, total), bf16)] * (tm_count - 1)
    outs += [
        jax.ShapeDtypeStruct(grads_in.shape, bf16),
        jax.ShapeDtypeStruct(tokens_in.shape, bf16),
    ]
    out_specs = [anywhere] * len(outs)
    if last:
        cut = round_up(shard // 2, 16)
        for _ in range(2):
            outs.append(jax.ShapeDtypeStruct((nz, cut, columns), bf16))
            outs.append(jax.ShapeDtypeStruct((nz, shard - cut + EXTRA, columns), bf16))
        out_specs += [pl.BlockSpec(memory_space=pltpu.VMEM)] * 4
    else:
        outs.append(jax.ShapeDtypeStruct((width, columns), f32))
        outs.append(jax.ShapeDtypeStruct((16, width), f32))
        out_specs += [anywhere] * 2
    args = list(facts) + list(pieces) + [tokens_in, grads_in] + list(blocks)
    aliases = {}
    if not first:
        args += list(before)
        aliases = {len(args) - 2: tm_count - 1, len(args) - 1: tm_count}
    rows = (tm_count, groups * group, frames, total)
    scratch = [
        pltpu.VMEM(rows, bf16),
        pltpu.VMEM((width, columns), bf16),
        pltpu.VMEM((dp_count, EXTRA, columns), bf16),
        pltpu.VMEM((tokens, width), bf16),
        pltpu.VMEM((tokens, width), f32),
        pltpu.VMEM((tokens, columns), bf16),
        pltpu.VMEM((tokens, columns), bf16),
        pltpu.VMEM(rows, bf16),
        pltpu.VMEM((width, columns), f32),
        pltpu.VMEM((tokens, 128), f32),
        pltpu.VMEM((16, width), f32),
        pltpu.VMEM((tm_count * frames, tokens // groups), f32),
        pltpu.SemaphoreType.DMA((6 * tm_count + 2 * dp_count + 14,)),
    ]
    return pl.pallas_call(
        functools.partial(
            chunk_kernel,
            tm_count,
            dp_count,
            frames,
            group,
            groups,
            patches_dev,
            offset,
            carry,
            first,
            last,
        ),
        out_shape=outs,
        in_specs=[pl.BlockSpec(memory_space=pltpu.SMEM)] * 3 + [anywhere] * (len(args) - 3),
        out_specs=out_specs,
        scratch_shapes=scratch,
        input_output_aliases=aliases,
        compiler_params=pltpu.CompilerParams(vmem_limit_bytes=vmem_limit),
    )(*args)


def partner(count, r):
    return [(i, i ^ r) for i in range(count)]


def body(
    video_tokens,
    norm_gain,
    norm_bias,
    qkv_weight,
    frame_counts,
    clip_starts,
    frame_kept,
    attended_grad,
):
    tm_count, dp_count = lax.axis_size("tm"), lax.axis_size("dp")
    nz = dp_count // CORES
    _, frames, patches, width = video_tokens.shape
    joined = attended_grad.shape[3]
    shard, columns = qkv_weight.shape
    patches_dev = -(-patches // tm_count)
    group = max(2, 128 // (frames * tm_count))
    chunks = chunk_sizes(patches_dev, group)
    dp = lax.axis_index("dp")

    def swap(array, r):
        return lax.ppermute(array, "tm", partner(tm_count, r))

    spare = ((0, tm_count * patches_dev - patches), (0, 0), (0, 0))
    tokens = jnp.pad(video_tokens[0].transpose(1, 0, 2), spare)
    upstream = jnp.pad(attended_grad[0].transpose(1, 0, 2), spare)
    offsets = [sum(chunks[:c]) for c in range(len(chunks))]

    def across(array, k):
        return lax.ppermute(array, "dp", partner(dp_count, k))

    blocks = [
        pack(tm_count, patches_dev, offset, size, tokens, upstream, *more)
        for offset, size, more in zip(offsets, chunks, ((qkv_weight, norm_gain, norm_bias), ()))
    ]
    own, early, late = blocks[0][0], list(blocks[0][1:]), blocks[1]
    along, bit = {0: own}, nz // 2
    while bit:
        along.update({k + bit: across(along[k], CORES * bit) for k in sorted(along)})
        bit //= 2
    along = [along[k] for k in range(nz)]
    early = [swap(part, r + 1) for r, part in enumerate(early)]
    along, early, late = lax.optimization_barrier((along, early, late))
    pieces = along + [across(jnp.stack(along), 1)]
    gathered = [early, [swap(part, r + 1) for r, part in enumerate(late)]]

    facts = (frame_counts, clip_starts, frame_kept)
    carry = patches_dev // CARRIED
    results, before = [], None
    for c in range(len(chunks)):
        blocks = gathered[c]
        first, last = c == 0, c == len(chunks) - 1
        got = chunk(
            tm_count,
            dp_count,
            group,
            patches_dev,
            offsets[c],
            carry,
            first,
            last,
            facts,
            pieces,
            (tokens, upstream, blocks),
            before,
        )
        leaving = got[: tm_count - 1]
        if first:
            leaving, gathered[1] = lax.optimization_barrier((leaving, gathered[1]))
        results.append([swap(part, r + 1) for r, part in enumerate(leaving)])
        mixed, grads = got[-6:-4] if last else got[-4:-2]
        before = list(got[tm_count - 1 : -4]) + [got[-2], got[-1], mixed, grads]
    keep, send = got[-4:-2], got[-2:]

    send, results[0] = lax.optimization_barrier((send, results[0]))
    others = [across(part, 1) for part in send]
    others, results[0] = lax.optimization_barrier((others, results[0]))
    halves = []
    for mine, other in zip(keep, others):
        left, bit = nz, 1
        half = mine.astype(f32) + other.astype(f32)
        while bit < nz:
            left //= 2
            gone = lax.optimization_barrier(half[left:].astype(bf16))
            got = across(gone, CORES * bit)
            half = half[:left] + got.astype(f32)
            bit *= 2
        halves.append(half[0])
    halves[0], results[-1] = lax.optimization_barrier((halves[0], results[-1]))
    summed = []
    for side, half in enumerate(halves):
        r = 1
        while r < tm_count:
            mine = lax.optimization_barrier(half.astype(bf16))
            got = swap(mine, r)
            if side == 0 and r == 1:
                got, results[-1] = lax.optimization_barrier((got, results[-1]))
            half = mine.astype(f32) + got.astype(f32)
            if side == 1 and 2 * r < tm_count:
                half += swap(mine, 2 * r).astype(f32) + swap(mine, 3 * r).astype(f32)
                r *= 2
            r *= 2
        summed.append(half)

    lead = chunks[0] - carry
    for start, size, blocks in zip((0, lead), (lead, patches_dev - lead), results):
        mixed, grads = unpack(tm_count, patches_dev, start, size, mixed, grads, blocks)
    attended = mixed[:patches].transpose(1, 0, 2)[None]
    tokens_grad = grads[:patches].transpose(1, 0, 2)[None]
    rest = shard - summed[0].shape[0]
    weight_total = jnp.concatenate([summed[0], summed[1][:rest]], axis=0)
    gain_total = lax.dynamic_slice(summed[1][rest], (dp * shard,), (shard,))
    bias_total = lax.dynamic_slice(summed[1][rest + 1], (dp * shard,), (shard,))
    return (attended, tokens_grad, weight_total, gain_total, bias_total)


def solution(mesh):
    placed = (
        P("dp", "tm", None, None),
        P("dp"),
        P("dp"),
        P("dp", None),
        P("dp"),
        P("dp", None),
        P("dp", None),
        P("dp", "tm", None, None),
    )
    return jax.shard_map(
        body,
        mesh=mesh,
        in_specs=placed,
        out_specs=(
            P("dp", "tm", None, None),
            P("dp", "tm", None, None),
            P("dp", None),
            P("dp"),
            P("dp"),
        ),
        check_vma=False,
    )
```

```python
import functools

import jax
import jax.numpy as jnp
from jax import lax
from jax.experimental import pallas as pl
from jax.experimental.pallas import tpu as pltpu
from jax.sharding import PartitionSpec as P

HEADS = 6
BLOCK = 16
CORES = 2
EXTRA = 8
CARRIED = 12

masked_value = -1e30
epsilon = 1e-05
vmem_limit = 56 * 1024 * 1024
f32 = jnp.float32
bf16 = jnp.bfloat16


def halving_order(count):
    order, bit = [0], count // 2
    while bit:
        order = order + [bit + k for k in order]
        bit //= 2
    return order


def round_up(value, step):
    return -(-value // step) * step


def chunk_sizes(patches_dev, group):
    whole = patches_dev // group
    second = (whole // 2) * group
    return [patches_dev - second, second]


anywhere = pl.BlockSpec(memory_space=pl.ANY)


def run_all(pairs, sems):
    copies = [pltpu.make_async_copy(a, b, sems.at[i]) for i, (a, b) in enumerate(pairs)]
    for copy in copies:
        copy.start()
    return copies


def pack_kernel(tm_count, patches_dev, offset, size, x_ref, grad_ref, *rest):
    sems = rest[-1]
    outs = rest[-tm_count:-1]
    width = x_ref.shape[2]
    me = lax.axis_index("tm")
    pairs = []
    for r in range(1, tm_count):
        place = pl.ds((me ^ r) * patches_dev + offset, size)
        pairs.append((x_ref.at[place], outs[r - 1].at[:, :, pl.ds(0, width)]))
        pairs.append(
            (grad_ref.at[place], outs[r - 1].at[:, :, pl.ds(width, grad_ref.shape[2])])
        )
    if len(rest) > tm_count:
        weight_ref, gain_ref, bias_ref, own_ref = rest[:4]
        shard, columns = weight_ref.shape
        pairs.append((weight_ref, own_ref.at[pl.ds(0, shard)]))
    copies = run_all(pairs, sems)
    if len(rest) > tm_count:
        row = lax.broadcasted_iota(jnp.int32, (EXTRA, columns), 0)
        owner = lax.broadcasted_iota(jnp.int32, (EXTRA, columns), 1) // shard
        spread = lambda ref: jnp.concatenate(
            [ref[...].astype(f32).reshape(1, shard)] * (columns // shard), axis=1
        )
        lines = jnp.where(row == 0, spread(gain_ref), jnp.where(row == 1, spread(bias_ref), 0.0))
        own_ref[shard:, :] = jnp.where(owner == lax.axis_index("dp"), lines, 0.0).astype(bf16)
    for copy in copies:
        copy.wait()


def pack(tm_count, patches_dev, offset, size, tokens, grads, weight=None, gain=None, bias=None):
    _, frames, width = tokens.shape
    total = width + grads.shape[2]
    in_vmem = pl.BlockSpec(memory_space=pltpu.VMEM)
    args, specs = [tokens, grads], [anywhere] * 2
    outs = [jax.ShapeDtypeStruct((size, frames, total), bf16)] * (tm_count - 1)
    if weight is not None:
        args += [weight, gain, bias]
        specs += [anywhere, in_vmem, in_vmem]
        shard, columns = weight.shape
        outs = [jax.ShapeDtypeStruct((shard + EXTRA, columns), bf16)] + outs
    return pl.pallas_call(
        functools.partial(pack_kernel, tm_count, patches_dev, offset, size),
        out_shape=outs,
        in_specs=specs,
        out_specs=[in_vmem] * len(outs),
        scratch_shapes=[pltpu.SemaphoreType.DMA((2 * tm_count,))],
        compiler_params=pltpu.CompilerParams(vmem_limit_bytes=vmem_limit),
    )(*args)


def unpack_kernel(tm_count, patches_dev, offset, size, *refs):
    ins = refs[2 : tm_count + 1]
    mixed_ref, grad_ref, held, sems, out_sems = refs[tm_count + 1 :]
    joined, width = mixed_ref.shape[2], grad_ref.shape[2]
    me = lax.axis_index("tm")
    arriving = run_all([(ins[r - 1], held.at[r - 1]) for r in range(1, tm_count)], sems)
    leaving = []
    for r in range(1, tm_count):
        place = pl.ds((me ^ r) * patches_dev + offset, size)
        arriving[r - 1].wait()
        for at, ref in ((0, mixed_ref), (joined, grad_ref)):
            copy = pltpu.make_async_copy(
                held.at[r - 1, :, :, pl.ds(at, ref.shape[2])],
                ref.at[place],
                out_sems.at[len(leaving)],
            )
            copy.start()
            leaving.append(copy)
    for copy in leaving:
        copy.wait()


def unpack(tm_count, patches_dev, offset, size, mixed, grads, blocks):
    return pl.pallas_call(
        functools.partial(unpack_kernel, tm_count, patches_dev, offset, size),
        out_shape=[
            jax.ShapeDtypeStruct(mixed.shape, bf16),
            jax.ShapeDtypeStruct(grads.shape, bf16),
        ],
        in_specs=[anywhere] * (tm_count + 1),
        out_specs=[anywhere] * 2,
        input_output_aliases={0: 0, 1: 1},
        scratch_shapes=[
            pltpu.VMEM((tm_count - 1,) + blocks[0].shape, bf16),
            pltpu.SemaphoreType.DMA((tm_count,)),
            pltpu.SemaphoreType.DMA((2 * tm_count,)),
        ],
        compiler_params=pltpu.CompilerParams(vmem_limit_bytes=vmem_limit),
    )(mixed, grads, *blocks)


def frame_facts(frame, count_ref, starts_ref, kept_ref):
    clip = jnp.zeros_like(frame)
    for b in range(1, starts_ref.shape[1]):
        clip = clip + jnp.where(frame >= b * BLOCK, starts_ref[0, b], 0)
    kept = jnp.zeros_like(frame)
    for g in range(kept_ref.shape[1]):
        kept = jnp.where(frame == g, kept_ref[0, g], kept)
    usable = (frame < count_ref[0]) & (kept == 1)
    return clip, usable


def chunk_kernel(
    tm_count,
    dp_count,
    frames,
    group,
    groups,
    patches_dev,
    offset,
    carry,
    first,
    last,
    count_ref,
    starts_ref,
    kept_ref,
    *rest,
):
    nz = dp_count // CORES
    rest = list(rest)
    take = lambda n: [rest.pop(0) for _ in range(n)]
    pieces = take(nz + 1)
    x_ref, grad_ref = take(2)
    sources = take(tm_count - 1)
    if not first:
        carried = take(tm_count - 1) if carry else []
        before, before_ends = take(2)
        take(2)
    outs = take(tm_count - 1)
    rests = take(tm_count - 1) if first and carry else []
    mixed_ref, tokens_ref = take(2)
    sums = take(4) if last else take(2)
    (xs, weight, extra, normed, standard, proj, pgrad, back, acc, ends, tails, allow, sems) = rest
    size = sources[0].shape[0]
    width = weight.shape[0]
    columns = weight.shape[1]
    joined = columns // 3
    tokens = groups * group * frames * tm_count
    span = group * frames
    shard = width // dp_count
    me = lax.axis_index("tm")
    dp = lax.axis_index("dp")
    z, core = dp // CORES, dp % CORES

    started = []

    def bring(src, dst):
        copy = pltpu.make_async_copy(src, dst, sems.at[len(started)])
        copy.start()
        started.append(copy)
        return copy

    mine = pl.ds(me * patches_dev + offset, size)
    kept = pl.ds(0, size)
    rows_in = [
        bring(x_ref.at[mine], xs.at[0, kept, :, pl.ds(0, width)]),
        bring(grad_ref.at[mine], xs.at[0, kept, :, pl.ds(width, joined)]),
    ]
    rows_in += [bring(sources[r - 1], xs.at[r, kept]) for r in range(1, tm_count)]
    weights_in, lines_in = [], []
    for side in range(CORES):
        for k in range(nz):
            owner = (z ^ k) * CORES + (core ^ side)
            piece = pieces[k] if side == 0 else pieces[nz].at[k]
            place = pl.ds(pl.multiple_of(owner * shard, shard), shard)
            weights_in.append(bring(piece.at[pl.ds(0, shard)], weight.at[place]))
            lines_in.append(bring(piece.at[pl.ds(shard, EXTRA)], extra.at[side * nz + k]))
    if not first:
        acc_in = [bring(before, acc), bring(before_ends, tails)]
    if xs.shape[1] > size:
        for r in range(tm_count):
            xs[r, size:] = jnp.zeros((xs.shape[1] - size,) + xs.shape[2:], bf16)

    row = lax.broadcasted_iota(jnp.int32, (tm_count * frames, tokens // groups), 0)
    lane = lax.broadcasted_iota(jnp.int32, (tm_count * frames, tokens // groups), 1)
    key_frame = (me ^ (row // frames)) * frames + row % frames
    query_frame = (me ^ (lane // span)) * frames + lane % frames
    key_clip, key_usable = frame_facts(key_frame, count_ref, starts_ref, kept_ref)
    query_clip, _ = frame_facts(query_frame, count_ref, starts_ref, kept_ref)
    ok = (key_clip == query_clip) & (key_usable | (key_frame == query_frame))
    allow[...] = jnp.where(ok, 1.0, 0.0)
    token = lax.broadcasted_iota(jnp.int32, (tokens // groups, 128), 0)
    token_frame = (me ^ (token // span)) * frames + token % frames
    token_valid = token_frame < count_ref[0]

    for copy in lines_in:
        copy.wait()
    gain = functools.reduce(
        lambda a, b: a + b, [extra[i, 0:1, :width].astype(f32) for i in range(dp_count)]
    )
    bias = functools.reduce(
        lambda a, b: a + b, [extra[i, 1:2, :width].astype(f32) for i in range(dp_count)]
    )
    for copy in rows_in:
        copy.wait()
    gone = []
    if not first:
        gone += [bring(ref, outs[r].at[pl.ds(0, carry)]) for r, ref in enumerate(carried)]

    unit = tokens // groups

    def token_rows(j, cut):
        rows = pl.ds(j * group, group)
        return jnp.concatenate(
            [xs[r, rows, :, cut].astype(f32).reshape(span, -1) for r in range(tm_count)], axis=0
        )

    def put_rows(j, cut, values):
        rows = pl.ds(j * group, group)
        for r in range(tm_count):
            block = values[r * span : (r + 1) * span].reshape(group, frames, -1)
            back[r, rows, :, cut] = block.astype(bf16)

    @pl.loop(0, groups, unroll=2)
    def _(j):
        x = token_rows(j, slice(0, width))
        centred = x - jnp.mean(x, axis=-1, keepdims=True)
        inverse = lax.rsqrt(jnp.mean(centred * centred, axis=-1, keepdims=True) + epsilon)
        std = centred * inverse
        at = pl.ds(pl.multiple_of(j * unit, unit), unit)
        standard[at, :] = std
        ends[at, :] = jnp.broadcast_to(inverse, (unit, 128))
        normed[at, :] = (std * gain + bias).astype(bf16)

    for copy in weights_in:
        copy.wait()
    cuts = [slice(at, min(at + 512, columns)) for at in range(0, columns, 512)]
    for cut in cuts:
        proj[:, cut] = jnp.dot(
            normed[...], weight[:, cut], preferred_element_type=f32
        ).astype(bf16)

    pairs = joined // 128
    wide = joined // HEADS
    scale = wide ** (-0.5)
    low = lax.broadcasted_iota(jnp.int32, (unit, 128), 1) < wide
    patch_lane = (lax.broadcasted_iota(jnp.int32, (1, unit), 1) // frames) % group

    def stack(block):
        zero = jnp.zeros_like(block)
        return jnp.concatenate(
            [jnp.where(low, block, zero), jnp.where(low, zero, block)], axis=0
        )

    def compact(full):
        parts = full.reshape(2, tm_count, group, frames, unit)
        got = parts[:, :, 0]
        for p in range(1, group):
            got = jnp.where(patch_lane == p, parts[:, :, p], got)
        return got.reshape(2, tm_count * frames, unit)

    def expand(small):
        small = small.reshape(2, tm_count, 1, frames, unit)
        pieces = [jnp.where(patch_lane == p, small, 0.0) for p in range(group)]
        return jnp.concatenate(pieces, axis=2).reshape(2 * unit, unit).astype(bf16)

    nt = (((1,), (1,)), ((), ()))
    tn = (((0,), (0,)), ((), ()))

    @pl.loop(0, groups, unroll=2)
    def _(j):
        at = pl.ds(pl.multiple_of(j * unit, unit), unit)
        allowed = allow[...] > 0.5
        every = range(pairs)
        cols = [slice(pair * 128, (pair + 1) * 128) for pair in every]
        cut = lambda part: [
            proj[at, part * joined + pair * 128 : part * joined + (pair + 1) * 128]
            for pair in every
        ]
        q2, k2, v2 = cut(0), cut(1), cut(2)
        up = [
            token_rows(j, slice(width + pair * 128, width + (pair + 1) * 128)) for pair in every
        ]
        up = [jnp.where(token_valid, u, 0.0).astype(bf16) for u in up]
        kcat, vcat = [stack(k) for k in k2], [stack(v) for v in v2]
        scores = [
            compact(lax.dot_general(kcat[i], q2[i], nt, preferred_element_type=f32))
            for i in every
        ]
        wgrad = [
            compact(lax.dot_general(vcat[i], up[i], nt, preferred_element_type=f32))
            for i in every
        ]
        probs = []
        for i in every:
            masked = jnp.where(allowed, scores[i] * scale, masked_value)
            shifted = jnp.exp(masked - jnp.max(masked, axis=1, keepdims=True))
            probs.append(shifted * (1.0 / jnp.sum(shifted, axis=1, keepdims=True)))
        full = [expand(p) for p in probs]
        sgrad = []
        for i in every:
            inner = jnp.sum(wgrad[i] * probs[i], axis=1, keepdims=True)
            sgrad.append(expand(probs[i] * (wgrad[i] - inner) * scale))
        for i in every:
            mixed = lax.dot_general(full[i], vcat[i], tn, preferred_element_type=f32)
            put_rows(j, cols[i], jnp.where(token_valid, mixed, 0.0))
            across = jnp.concatenate([full[i][:unit], full[i][unit:]], axis=1)
            value_grad = jnp.dot(across, stack(up[i]), preferred_element_type=f32)
            query_grad = lax.dot_general(sgrad[i], kcat[i], tn, preferred_element_type=f32)
            sacross = jnp.concatenate([sgrad[i][:unit], sgrad[i][unit:]], axis=1)
            key_grad = jnp.dot(sacross, stack(q2[i]), preferred_element_type=f32)
            for part, value in enumerate((query_grad, key_grad, value_grad)):
                place = slice(part * joined + i * 128, part * joined + (i + 1) * 128)
                pgrad[at, place] = value.astype(bf16)

    if not first:
        for copy in acc_in:
            copy.wait()
    else:
        tails[...] = jnp.zeros_like(tails)
    for cut in cuts:
        share = lax.dot_general(normed[...], pgrad[:, cut], tn, preferred_element_type=f32)
        if first:
            acc[:, cut] = share
        else:
            acc[:, cut] += share

    if not last:
        gone.append(bring(acc, sums[0]))
    else:
        cut = sums[0].shape[1]
        for k, far in enumerate(halving_order(nz)):
            owner = (z ^ far) * CORES
            for refs, side in ((sums[:2], core), (sums[2:], 1 - core)):
                start = pl.multiple_of((owner + side) * shard, shard)
                refs[0][k] = acc[pl.ds(start, cut), :].astype(bf16)
                refs[1][k, : shard - cut, :] = acc[
                    pl.ds(pl.multiple_of(start + cut, 16), shard - cut), :
                ].astype(bf16)
    normed[...] = lax.dot_general(
        pgrad[...], weight[...], nt, preferred_element_type=f32
    ).astype(bf16)

    def finish(j):
        at = pl.ds(pl.multiple_of(j * unit, unit), unit)
        ngrad = normed[at, :].astype(f32)
        std = standard[at, :]
        product = ngrad * std
        tails[0:8, :] += jnp.sum(product.reshape(unit // 8, 8, width), axis=0)
        tails[8:16, :] += jnp.sum(ngrad.reshape(unit // 8, 8, width), axis=0)
        scaled = ngrad * gain
        grad = ends[at, 0:1] * (
            scaled
            - jnp.mean(scaled, axis=-1, keepdims=True)
            - std * jnp.mean(product * gain, axis=-1, keepdims=True)
        )
        put_rows(j, slice(joined, columns), grad)

    middle = (groups + 1) // 2
    for low_group, high_group in ((0, middle), (middle, groups)):
        pl.loop(low_group, high_group, unroll=2)(finish)
        start = low_group * group
        count = min(high_group * group, size) - start
        here, there = pl.ds(start, count), pl.ds(me * patches_dev + offset + start, count)
        now = max(0, min(start + count, size - carry) - start) if first else count
        shift = 0 if first else carry
        for r in range(1, tm_count):
            if now:
                part = back.at[r, pl.ds(start, now)]
                gone.append(bring(part, outs[r - 1].at[pl.ds(start + shift, now)]))
            if now < count:
                part = back.at[r, pl.ds(start + now, count - now)]
                there_rest = pl.ds(start + now - (size - carry), count - now)
                gone.append(bring(part, rests[r - 1].at[there_rest]))
        gone.append(bring(back.at[0, here, :, pl.ds(0, joined)], mixed_ref.at[there]))
        gone.append(bring(back.at[0, here, :, pl.ds(joined, width)], tokens_ref.at[there]))
    if not last:
        gone.append(bring(tails, sums[1]))
    else:
        cut = sums[0].shape[1]
        extra_rows = jnp.concatenate(
            [
                jnp.sum(tails[0:8, :], axis=0, keepdims=True),
                jnp.sum(tails[8:16, :], axis=0, keepdims=True),
                jnp.zeros((EXTRA - 2, width), f32),
            ],
            axis=0,
        ).astype(bf16)
        for k in range(nz):
            for ref in (sums[1], sums[3]):
                ref[k, shard - cut :, :width] = extra_rows
                ref[k, shard - cut :, width:] = jnp.zeros((EXTRA, columns - width), bf16)
    for copy in gone:
        copy.wait()


def chunk(
    tm_count,
    dp_count,
    group,
    patches_dev,
    offset,
    carry,
    first,
    last,
    facts,
    pieces,
    sources,
    before,
):
    tokens_in, grads_in, blocks = sources
    size, frames, total = blocks[0].shape
    shard, columns = pieces[0].shape[0] - EXTRA, pieces[0].shape[1]
    width = shard * dp_count
    groups = -(-size // group)
    tokens = groups * group * frames * tm_count
    nz = dp_count // CORES
    leaving = size - carry if first else size + carry
    outs = [jax.ShapeDtypeStruct((leaving, frames, total), bf16)] * (tm_count - 1)
    if first and carry:
        outs += [jax.ShapeDtypeStruct((carry, frames, total), bf16)] * (tm_count - 1)
    outs += [
        jax.ShapeDtypeStruct(grads_in.shape, bf16),
        jax.ShapeDtypeStruct(tokens_in.shape, bf16),
    ]
    out_specs = [anywhere] * len(outs)
    if last:
        cut = round_up(shard // 2, 16)
        for _ in range(2):
            outs.append(jax.ShapeDtypeStruct((nz, cut, columns), bf16))
            outs.append(jax.ShapeDtypeStruct((nz, shard - cut + EXTRA, columns), bf16))
        out_specs += [pl.BlockSpec(memory_space=pltpu.VMEM)] * 4
    else:
        outs.append(jax.ShapeDtypeStruct((width, columns), f32))
        outs.append(jax.ShapeDtypeStruct((16, width), f32))
        out_specs += [anywhere] * 2
    args = list(facts) + list(pieces) + [tokens_in, grads_in] + list(blocks)
    aliases = {}
    if not first:
        args += list(before)
        aliases = {len(args) - 2: tm_count - 1, len(args) - 1: tm_count}
    rows = (tm_count, groups * group, frames, total)
    scratch = [
        pltpu.VMEM(rows, bf16),
        pltpu.VMEM((width, columns), bf16),
        pltpu.VMEM((dp_count, EXTRA, columns), bf16),
        pltpu.VMEM((tokens, width), bf16),
        pltpu.VMEM((tokens, width), f32),
        pltpu.VMEM((tokens, columns), bf16),
        pltpu.VMEM((tokens, columns), bf16),
        pltpu.VMEM(rows, bf16),
        pltpu.VMEM((width, columns), f32),
        pltpu.VMEM((tokens, 128), f32),
        pltpu.VMEM((16, width), f32),
        pltpu.VMEM((tm_count * frames, tokens // groups), f32),
        pltpu.SemaphoreType.DMA((6 * tm_count + 2 * dp_count + 14,)),
    ]
    return pl.pallas_call(
        functools.partial(
            chunk_kernel,
            tm_count,
            dp_count,
            frames,
            group,
            groups,
            patches_dev,
            offset,
            carry,
            first,
            last,
        ),
        out_shape=outs,
        in_specs=[pl.BlockSpec(memory_space=pltpu.SMEM)] * 3 + [anywhere] * (len(args) - 3),
        out_specs=out_specs,
        scratch_shapes=scratch,
        input_output_aliases=aliases,
        compiler_params=pltpu.CompilerParams(vmem_limit_bytes=vmem_limit),
    )(*args)


def partner(count, r):
    return [(i, i ^ r) for i in range(count)]


def body(
    video_tokens,
    norm_gain,
    norm_bias,
    qkv_weight,
    frame_counts,
    clip_starts,
    frame_kept,
    attended_grad,
):
    tm_count, dp_count = lax.axis_size("tm"), lax.axis_size("dp")
    nz = dp_count // CORES
    _, frames, patches, width = video_tokens.shape
    joined = attended_grad.shape[3]
    shard, columns = qkv_weight.shape
    patches_dev = -(-patches // tm_count)
    group = max(2, 128 // (frames * tm_count))
    chunks = chunk_sizes(patches_dev, group)
    dp = lax.axis_index("dp")

    def swap(array, r):
        return lax.ppermute(array, "tm", partner(tm_count, r))

    spare = ((0, tm_count * patches_dev - patches), (0, 0), (0, 0))
    tokens = jnp.pad(video_tokens[0].transpose(1, 0, 2), spare)
    upstream = jnp.pad(attended_grad[0].transpose(1, 0, 2), spare)
    offsets = [sum(chunks[:c]) for c in range(len(chunks))]

    def across(array, k):
        return lax.ppermute(array, "dp", partner(dp_count, k))

    blocks = [
        pack(tm_count, patches_dev, offset, size, tokens, upstream, *more)
        for offset, size, more in zip(offsets, chunks, ((qkv_weight, norm_gain, norm_bias), ()))
    ]
    own, early, late = blocks[0][0], list(blocks[0][1:]), blocks[1]
    along, bit = {0: own}, nz // 2
    while bit:
        along.update({k + bit: across(along[k], CORES * bit) for k in sorted(along)})
        bit //= 2
    along = [along[k] for k in range(nz)]
    early = [swap(part, r + 1) for r, part in enumerate(early)]
    along, early, late = lax.optimization_barrier((along, early, late))
    pieces = along + [across(jnp.stack(along), 1)]
    gathered = [early, [swap(part, r + 1) for r, part in enumerate(late)]]

    facts = (frame_counts, clip_starts, frame_kept)
    carry = patches_dev // CARRIED
    results, before = [], None
    for c in range(len(chunks)):
        blocks = gathered[c]
        first, last = c == 0, c == len(chunks) - 1
        got = chunk(
            tm_count,
            dp_count,
            group,
            patches_dev,
            offsets[c],
            carry,
            first,
            last,
            facts,
            pieces,
            (tokens, upstream, blocks),
            before,
        )
        leaving = got[: tm_count - 1]
        if first:
            leaving, gathered[1] = lax.optimization_barrier((leaving, gathered[1]))
        results.append([swap(part, r + 1) for r, part in enumerate(leaving)])
        mixed, grads = got[-6:-4] if last else got[-4:-2]
        before = list(got[tm_count - 1 : -4]) + [got[-2], got[-1], mixed, grads]
    keep, send = got[-4:-2], got[-2:]

    send, results[0] = lax.optimization_barrier((send, results[0]))
    others = [across(part, 1) for part in send]
    others, results[0] = lax.optimization_barrier((others, results[0]))
    halves = []
    for mine, other in zip(keep, others):
        left, bit = nz, 1
        half = mine.astype(f32) + other.astype(f32)
        while bit < nz:
            left //= 2
            gone = lax.optimization_barrier(half[left:].astype(bf16))
            got = across(gone, CORES * bit)
            half = half[:left] + got.astype(f32)
            bit *= 2
        halves.append(half[0])
    halves[0], results[-1][:-1] = lax.optimization_barrier((halves[0], results[-1][:-1]))
    summed = []
    for side, half in enumerate(halves):
        r = 1
        while r < tm_count:
            mine = lax.optimization_barrier(half.astype(bf16))
            got = swap(mine, r)
            if side == 0 and r == 1:
                got, results[-1] = lax.optimization_barrier((got, results[-1]))
            half = mine.astype(f32) + got.astype(f32)
            if side == 1 and 2 * r < tm_count:
                half += swap(mine, 2 * r).astype(f32) + swap(mine, 3 * r).astype(f32)
                r *= 2
            r *= 2
        summed.append(half)

    lead = chunks[0] - carry
    for start, size, blocks in zip((0, lead), (lead, patches_dev - lead), results):
        mixed, grads = unpack(tm_count, patches_dev, start, size, mixed, grads, blocks)
    attended = mixed[:patches].transpose(1, 0, 2)[None]
    tokens_grad = grads[:patches].transpose(1, 0, 2)[None]
    rest = shard - summed[0].shape[0]
    weight_total = jnp.concatenate([summed[0], summed[1][:rest]], axis=0)
    gain_total = lax.dynamic_slice(summed[1][rest], (dp * shard,), (shard,))
    bias_total = lax.dynamic_slice(summed[1][rest + 1], (dp * shard,), (shard,))
    return (attended, tokens_grad, weight_total, gain_total, bias_total)


def solution(mesh):
    placed = (
        P("dp", "tm", None, None),
        P("dp"),
        P("dp"),
        P("dp", None),
        P("dp"),
        P("dp", None),
        P("dp", None),
        P("dp", "tm", None, None),
    )
    return jax.shard_map(
        body,
        mesh=mesh,
        in_specs=placed,
        out_specs=(
            P("dp", "tm", None, None),
            P("dp", "tm", None, None),
            P("dp", None),
            P("dp"),
            P("dp"),
        ),
        check_vma=False,
    )
```
